512 devices in a mesh: lat: 16 (over z_lo, core), lon: 32 (over y, z_hi, x).
Axes of the slice: x: 4, y: 4, z: 16 (z_hi: 2, z_lo: 8; z = z_hi * 8 + z_lo), core: 2. Of those that a mesh axis runs over, the one named last changes fastest.
Arguments:
- fields: bfloat16 [4, 96, 384, 512], P(None, 'lat', 'lon'), may hold values from -8 to 8
- qkv_weight: bfloat16 [512, 1536], replicated
- out_weight: bfloat16 [512, 512], replicated, may hold values from -0.75 to 0.75
- cotangent: bfloat16 [4, 96, 384, 512], P(None, 'lat', 'lon'), may hold values from -6 to 6
Outputs:
- layer_out: bfloat16 [4, 96, 384, 512], P(None, 'lat', 'lon')
- grad_fields: bfloat16 [4, 96, 384, 512], P(None, 'lat', 'lon')
- grad_out_weight: float32 [512, 512], P('lat', 'lon')
The draws below stay inside these ranges and needn't reach their ends.
All inputs are finite; a program needn't handle non-finite values.
Results may differ from the reference program's by a relative error of at most 0.017.
The reference program's roundings to bfloat16 on the way count: a program that leaves them out, or rounds other values in their place, can miss the bound.
Values may be sent and summed in bfloat16 or wider, within the bound.
A program may use at most 64 MiB of HBM per device.

```python
import math
import jax
import jax.numpy as jnp
from jax import lax

D = 512
HEAD_DIM = 64
LEV = 4
WLEV = 2
WLAT = 6
WLON = 12
NLAT = 96
NLON = 384


def draw_fields(key, part):
    key = jax.random.fold_in(key, 11)
    grid_shape = (LEV, NLAT, NLON, D)
    drawn = jax.random.truncated_normal(key, -4.0, 4.0, grid_shape, jnp.float32)
    return drawn.astype(jnp.bfloat16)


def draw_qkv_weight(key, part):
    key = jax.random.fold_in(key, 23)
    drawn = jax.random.truncated_normal(key, -4.0, 4.0, (D, 3 * D), jnp.float32) * D ** (-0.5)
    return drawn.astype(jnp.bfloat16)


def shard_levels(rng, dims, cuts, smallest, top_value):
    factor_of = 1.0
    for axis_at, blocks in cuts:
        draws = jax.random.uniform(jax.random.fold_in(jax.random.fold_in(rng, 6), axis_at), (blocks,), jnp.float32, smallest / len(cuts), top_value / len(cuts))
        factor_of = factor_of * jnp.repeat(jnp.exp(draws), dims[axis_at] // blocks).reshape((-1,) + (1,) * (len(dims) - 1 - axis_at))
    return factor_of


def gaussian(stream_key, dims, spread, limit, cuts=(), held_as=jnp.bfloat16):
    loudness = shard_levels(stream_key, dims, cuts, -0.22, 0.18) if cuts else 1.0
    values = jax.random.normal(stream_key, dims, jnp.float32) * spread * loudness
    return jnp.minimum(jnp.maximum(values, -limit), limit).astype(held_as)


def setup_inputs(seed: int = 0) -> dict:
    arg_keys = jax.random.split(jax.random.key(seed), 5)
    fields = draw_fields(jax.random.fold_in(arg_keys[4], 71), 0)
    qkv_weight = draw_qkv_weight(jax.random.fold_in(arg_keys[4], 71), 0)
    out_weight = gaussian(arg_keys[2], (D, D), (D // 8) ** -0.5, 0.75)
    cotangent = gaussian(arg_keys[3], (LEV, NLAT, NLON, D), 1.0, 6.0, ((1, 16), (2, 32)))
    return dict(fields=fields, qkv_weight=qkv_weight, out_weight=out_weight, cotangent=cotangent)


EPSILON = 1e-05
MASK_FILL = -1e+30

def normalize(fields):
    widened = fields.astype(jnp.float32)
    centred = widened - lax.optimization_barrier(jnp.mean(widened, -1, keepdims=True))
    inverse = lax.rsqrt(lax.optimization_barrier(jnp.mean(centred * centred, -1, keepdims=True)) + EPSILON)
    normed_hat = centred * inverse
    return (normed_hat.astype(jnp.bfloat16), normed_hat, inverse)

def normalize_back(grad_normed, normed_hat, inverse):
    widened = grad_normed.astype(jnp.float32)
    centred = widened - lax.optimization_barrier(jnp.mean(widened, -1, keepdims=True))
    return inverse * (centred - normed_hat * lax.optimization_barrier(jnp.mean(widened * normed_hat, -1, keepdims=True)))

def to_windows(blocks):
    lev_count, lat_rows, lon_cols, channels = blocks.shape
    tiled = blocks.reshape(lev_count // WLEV, WLEV, lat_rows // WLAT, WLAT, lon_cols // WLON, WLON, channels)
    return tiled.transpose(0, 2, 4, 1, 3, 5, 6).reshape(-1, WLEV * WLAT * WLON, channels)

def from_windows(windows, grid_shape):
    lev_count, lat_rows, lon_cols, channels = grid_shape
    tiled = windows.reshape(lev_count // WLEV, lat_rows // WLAT, lon_cols // WLON, WLEV, WLAT, WLON, channels)
    return tiled.transpose(0, 3, 1, 4, 2, 5, 6).reshape(grid_shape)

def region_ids(lev_count, lat_global, lat_total, lon_cols):
    levels = jnp.arange(lev_count, dtype=jnp.int32)
    lev_region = (levels >= lev_count - WLEV).astype(jnp.int32) + (levels >= lev_count - WLEV // 2).astype(jnp.int32)
    lat_region = (lat_global >= lat_total - WLAT).astype(jnp.int32) + (lat_global >= lat_total - WLAT // 2).astype(jnp.int32)
    return 3 * lev_region[:, None, None] + lat_region[None, :, None] + jnp.zeros((1, 1, lon_cols), jnp.int32)

def product(form, left, right):
    return jnp.einsum(form, left.astype(jnp.float32), right.astype(jnp.float32), precision=lax.Precision.HIGHEST)

def window_forward(windows, allowed, qkv_weight, out_weight):
    win_count, win_tokens, channels = windows.shape
    head_count = channels // HEAD_DIM
    projected = jnp.dot(windows.reshape(-1, channels), qkv_weight, preferred_element_type=jnp.float32).astype(jnp.bfloat16)
    projected = projected.reshape(win_count, win_tokens, 3, head_count, HEAD_DIM)
    queries = projected[:, :, 0]
    key_rows = projected[:, :, 1]
    values = projected[:, :, 2]
    scores = product('nqhe,nkhe->nhqk', queries, key_rows) * HEAD_DIM ** (-0.5)
    scores = jnp.where(allowed[:, None], scores, MASK_FILL)
    lifted = jnp.exp(scores - lax.optimization_barrier(jnp.max(scores, -1, keepdims=True)))
    attend = lifted / lax.optimization_barrier(jnp.sum(lifted, -1, keepdims=True))
    attend_low = attend.astype(jnp.bfloat16)
    context = product('nhqk,nkhe->nqhe', attend_low, values).astype(jnp.bfloat16).reshape(-1, channels)
    output = jnp.dot(context, out_weight, preferred_element_type=jnp.float32).astype(jnp.bfloat16)
    return (output, (queries, key_rows, values, attend, attend_low, context))

def window_backward(saved, grad_rows, qkv_weight, out_weight):
    queries, key_rows, values, attend, attend_low, context = saved
    channels = context.shape[1]
    grad_context = lax.dot_general(grad_rows, out_weight, (((1,), (1,)), ((), ())), preferred_element_type=jnp.float32)
    grad_context = grad_context.astype(jnp.bfloat16).reshape(queries.shape)
    grad_attend = product('nqhe,nkhe->nhqk', grad_context, values)
    grad_scores = attend * (grad_attend - lax.optimization_barrier(jnp.sum(attend * grad_attend, -1, keepdims=True))) * HEAD_DIM ** (-0.5)
    grad_scores = grad_scores.astype(jnp.bfloat16)
    grad_query = product('nhqk,nkhe->nqhe', grad_scores, key_rows)
    grad_keys = product('nhqk,nqhe->nkhe', grad_scores, queries)
    grad_values = product('nhqk,nqhe->nkhe', attend_low, grad_context)
    grad_proj = jnp.stack([grad_query, grad_keys, grad_values], 2).astype(jnp.bfloat16).reshape(-1, 3 * channels)
    grad_shifted = lax.dot_general(grad_proj, qkv_weight, (((1,), (1,)), ((), ())), preferred_element_type=jnp.float32)
    return grad_shifted.astype(jnp.bfloat16)

def reference(fields, qkv_weight, out_weight, cotangent):
    channels = fields.shape[3]
    normed, normed_hat, inverse = normalize(fields)
    offsets = (-(WLEV // 2), -(WLAT // 2), -(WLON // 2))
    returns = (WLEV // 2, WLAT // 2, WLON // 2)
    shifted = jnp.roll(normed, offsets, (0, 1, 2))
    shifted_cot = jnp.roll(cotangent, offsets, (0, 1, 2))
    region = region_ids(LEV, jnp.arange(NLAT, dtype=jnp.int32), NLAT, NLON)
    band_count = NLAT // WLAT

    def band_view(grid):
        return grid.reshape(LEV, band_count, WLAT, NLON, grid.shape[3]).transpose(1, 0, 2, 3, 4)

    def unband(stacked):
        return stacked.transpose(1, 0, 2, 3, 4).reshape(LEV, NLAT, NLON, stacked.shape[4])

    def band_pass(items):
        band_fields, band_cot, band_region = items
        region_win = to_windows(band_region)[..., 0]
        allowed = region_win[:, :, None] == region_win[:, None, :]
        output, saved = window_forward(to_windows(band_fields), allowed, qkv_weight, out_weight)
        grad_rows = to_windows(band_cot).reshape(-1, channels)
        grad_shifted = window_backward(saved, grad_rows, qkv_weight, out_weight)
        term = lax.dot_general(saved[5], grad_rows, (((0,), (0,)), ((), ())), preferred_element_type=jnp.float32)
        band_shape = band_fields.shape
        return (from_windows(output, band_shape), from_windows(grad_shifted.reshape(output.shape[0] // (WLEV * WLAT * WLON), WLEV * WLAT * WLON, channels), band_shape), term)
    results = lax.map(band_pass, (band_view(shifted), band_view(shifted_cot), band_view(region[..., None])))
    branch_back = jnp.roll(unband(results[0]), returns, (0, 1, 2))
    grad_normed = jnp.roll(unband(results[1]), returns, (0, 1, 2))
    layer_out = (fields.astype(jnp.float32) + branch_back.astype(jnp.float32)).astype(jnp.bfloat16)
    grad_fields = (cotangent.astype(jnp.float32) + normalize_back(grad_normed, normed_hat, inverse)).astype(jnp.bfloat16)
    grad_out_weight = lax.optimization_barrier(jnp.sum(results[2], 0)) * (1.0 / math.sqrt(LEV * NLAT * NLON))
    return (layer_out, grad_fields, grad_out_weight)
```

```python
import functools
import math

import jax
import jax.numpy as jnp
from jax import lax
from jax.experimental import pallas as pl
from jax.experimental.pallas import tpu as pltpu
from jax.sharding import PartitionSpec as P

MESH = pl.DeviceIdType.MESH
EPSILON = 1e-05
MASK_FILL = -1e30
BF = jnp.bfloat16
F32 = jnp.float32
D = 512
LATS = 16
LONS = 32
BLOCK = (16, 1152)


def dot(a, b, ca=1, cb=0):
    return lax.dot_general(a, b, (((ca,), (cb,)), ((), ())), preferred_element_type=F32)


def iota(shape, dim):
    return lax.broadcasted_iota(jnp.int32, shape, dim)


def ones_where(cond):
    return jnp.where(cond, 1.0, 0.0).astype(BF)


def z_quarter(lat, lon, back):
    zl = lat // 2
    h = (lon // 4) % 2
    low = (zl + 4) % 8
    wraps = 1 - zl // 4 if back else zl // 4
    return low * 2 + lat % 2, lon + ((h + wraps) % 2 - h) * 4


def moved(lat, lon, cond, back):
    qlat, qlon = z_quarter(lat, lon, back)
    return jnp.where(cond, qlat, lat), jnp.where(cond, qlon, lon)


def block_host(lat, lon, r, c, p):
    kb = lon if c == 1 else (lon + LONS - 1) % LONS
    crossing = kb % 4 == 3
    q = (1 - r) * 2 + (1 - c)
    east = (kb + 1) % LONS
    if p == 0 and r == 1:
        hlat, hlon, pos = lat, kb, q
    elif p == 0:
        edge = lat == 0
        hlat = jnp.where(edge, 0, lat - 1)
        hlon = jnp.where(edge, east, kb)
        pos = jnp.where(edge, 4 + q - 2, q)
    elif r == 0:
        hlat, hlon, pos = lat, east, 4 + q
    else:
        edge = lat == LATS - 1
        hlat = jnp.where(edge, LATS - 1, lat + 1)
        hlon = jnp.where(edge, kb, east)
        pos = jnp.where(edge, q + 2, 4 + q)
    hlat, hlon = moved(hlat, hlon, crossing, False)
    return hlat, hlon, pos


def virtual_host(lat, lon, slot):
    x = lon % 4
    crossing = x == jnp.where(slot == 0, 3, 0)
    return moved(lat, lon, crossing, True)


def inbox_source(lat, lon, slot, q):
    va, vb = virtual_host(lat, lon, slot)
    south, east = q // 2, q % 2
    if slot == 0:
        edge = va == LATS - 1
        if south == 0:
            slat, r, p = va, 1, 0
        else:
            slat = jnp.where(edge, va, va + 1)
            r = jnp.where(edge, 1, 0)
            p = jnp.where(edge, 1, 0)
        slon = (vb + east) % LONS
    else:
        edge = va == 0
        if south == 1:
            slat, r, p = va, 0, 1
        else:
            slat = jnp.where(edge, va, va - 1)
            r = jnp.where(edge, 0, 1)
            p = jnp.where(edge, 0, 1)
        slon = (vb + LONS - 1 + east) % LONS
    return slat, slon, (r * 2 + (1 - east)) * 2 + p


def grid_row(m):
    tail = m >= 256
    k = jnp.where(tail, (m - 256) >> 2, m >> 5)
    t = jnp.where(tail, 32 + ((m - 256) & 3), m & 31)
    r, c, p = k >> 2, (k >> 1) & 1, k & 1
    l2 = jnp.where(t >= 18, 1, 0)
    t = t - 18 * l2
    r3 = jnp.where(t >= 6, 1, 0) + jnp.where(t >= 12, 1, 0)
    lev = (1 + 2 * p + l2) & 3
    return (lev * 6 + 3 * r + r3) * 16 + 6 * c + t - 6 * r3


def tail_map(count, j):
    rows = iota((4 * count, 1), 0)
    return ones_where((rows >> 2) * 16 + 4 * j + (rows & 3) == iota((4 * count, 16 * count), 1))


def store_blocks(ref, base, rows, count):
    for k in range(count):
        ref[base + k, :, 0:512] = rows[32 * k : 32 * k + 16]
        ref[base + k, :, 512:1024] = rows[32 * k + 16 : 32 * k + 32]
    tails = rows[32 * count :]
    packed = sum(
        dot(tail_map(count, j), tails[:, 128 * j : 128 * j + 128], 0, 0) for j in range(4)
    ).astype(BF)
    for k in range(count):
        ref[base + k, :, 1024:1152] = packed[16 * k : 16 * k + 16]


def load_blocks(ref, base, count):
    main = []
    for k in range(count):
        main += [ref[base + k, :, 0:512], ref[base + k, :, 512:1024]]
    packed = jnp.concatenate([ref[base + k, :, 1024:1152] for k in range(count)], 0)
    tails = jnp.concatenate([dot(tail_map(count, j), packed) for j in range(4)], 1).astype(BF)
    return jnp.concatenate(main + [tails], 0)


def group_ids(m, slot, edge):
    tail = m >= 128
    q = jnp.where(tail, (m - 128) >> 2, m >> 5)
    t = jnp.where(tail, 32 + ((m - 128) & 3), m & 31)
    l2 = jnp.where(t >= 18, 1, 0)
    south = q >> 1
    first = jnp.where(edge, south * (1 + l2), 0)
    second = jnp.where(edge, jnp.where(south == 0, 2, l2), l2)
    return jnp.where(slot == 0, first, second)


def kernel(
    factor,
    fields_ref, qkv_hbm, out_hbm, cot_ref,
    layer_ref, grad_ref, dw_ref,
    pad, hat, inv, qkv_w, out_w,
    out_f, out_c, in_f, in_c, res_b, res_g, ret_b, ret_g,
    proj, att, ctx, gproj, acc,
    a_src, a_dst, b_src, b_dst, c_src, c_dst, d_src, d_dst,
    w_sem, sf, sc, sb, sg, rf, rc, rb, rg,
    a_sem, bs_sem, br_sem, cs_sem, cr_sem, ds_sem, dr_sem,
):
    lat = lax.axis_index("lat")
    lon = lax.axis_index("lon")
    core, zl = lat % 2, lat // 2
    y, h, x = lon // 8, (lon // 4) % 2, lon % 4
    z = h * 8 + zl
    yx = y * 4 + x
    collector = zl // 2 == x

    def at(y_, x_, z_, c_):
        return ((z_ % 8) * 2 + c_, y_ * 8 + (z_ // 8) * 4 + x_)

    def same(dlat, dlon):
        return jnp.logical_and(dlat == lat, dlon == lon)

    load_w = [
        pltpu.make_async_copy(qkv_hbm, qkv_w, w_sem.at[0]),
        pltpu.make_async_copy(out_hbm, out_w, w_sem.at[1]),
    ]
    for copy in load_w:
        copy.start()

    hosts = [block_host(lat, lon, k >> 2, (k >> 1) & 1, k & 1) for k in range(8)]
    sources = [inbox_source(lat, lon, i // 4, i % 4) for i in range(8)]

    barrier = pltpu.get_barrier_semaphore()

    def tell(dlat, dlon):
        pl.semaphore_signal(barrier, inc=1, device_id=(dlat, dlon), device_id_type=MESH)

    due = jnp.int32(16)
    for slat, slon, _ in sources:
        pl.when(jnp.logical_not(same(slat, slon)))(functools.partial(tell, slat, slon))
    for hlat, hlon, _ in hosts:
        due = due + jnp.where(same(hlat, hlon), 0, 1)
    tell(zl * 2 + 1 - core, lon)

    def tell_plane(d, carry):
        partner = yx ^ d
        tell(*at(partner // 4, partner % 4, z, core))
        return carry

    lax.fori_loop(1, 16, tell_plane, 0)

    @pl.when(collector)
    def _():
        def tell_ring(d, carry):
            tell(*at(y, x, z ^ d, core))
            return carry

        lax.fori_loop(1, 16, tell_ring, 0)

    due = due + jnp.where(collector, 3, 4)

    pad[...] = jnp.zeros_like(pad)
    pad[0, :, 0:12, :] = fields_ref[...]
    pad[1, :, 0:12, :] = cot_ref[...]
    wide = pad[0].reshape(384, D).astype(F32)
    centred = wide - jnp.mean(wide, -1, keepdims=True)
    inverse = lax.rsqrt(jnp.mean(centred * centred, -1, keepdims=True) + EPSILON)
    normed_hat = centred * inverse
    hat[...] = normed_hat
    inv[...] = inverse
    to_blocks = ones_where(grid_row(iota((288, 1), 0)) == iota((288, 384), 1))
    store_blocks(out_f, 0, dot(to_blocks, normed_hat.astype(BF)).astype(BF), 8)
    store_blocks(out_c, 0, dot(to_blocks, pad[1].reshape(384, D)).astype(BF), 8)

    pl.semaphore_wait(barrier, due)

    def send(src, dst, send_sems, recv_sems, i, dlat, dlon, j):
        here = same(dlat, dlon)

        @pl.when(here)
        def _():
            pltpu.make_async_copy(src.at[i], dst.at[j], recv_sems.at[j]).start()

        @pl.when(jnp.logical_not(here))
        def _():
            pltpu.make_async_remote_copy(
                src_ref=src.at[i], dst_ref=dst.at[j], send_sem=send_sems.at[i], recv_sem=recv_sems.at[j],
                device_id=(dlat, dlon), device_id_type=MESH,
            ).start()

    def landed(dst, sems, j):
        pltpu.make_async_copy(dst.at[j], dst.at[j], sems.at[j]).wait()

    def sent(src, sems, i, dlat, dlon):
        @pl.when(jnp.logical_not(same(dlat, dlon)))
        def _():
            pltpu.make_async_copy(src.at[i], src.at[i], sems.at[i]).wait()

    for src, dst, ss, rs in ((out_f, in_f, sf, rf), (out_c, in_c, sc, rc)):
        for k, (hlat, hlon, pos) in enumerate(hosts):
            send(src, dst, ss, rs, k, hlat, hlon, pos)

    for copy in load_w:
        copy.wait()

    first_half = iota((144, 128), 1) < 64

    def halves(pair):
        zero = jnp.zeros_like(pair)
        return jnp.concatenate([jnp.where(first_half, pair, zero), jnp.where(first_half, zero, pair)], 0)

    def merge(stacked):
        return jnp.where(first_half, stacked[:144], stacked[144:])

    def send_back(slot, src, dst, ss, rs):
        for s in range(2):
            @pl.when(slot == s)
            def _():
                for q in range(4):
                    slat, slon, k = sources[s * 4 + q]
                    send(src, dst, ss, rs, s * 4 + q, slat, slon, k)

    def window(i, carry):
        slot = jnp.where(x == 0, i, 1 - i)
        va, _ = virtual_host(lat, lon, slot)
        edge = va == jnp.where(slot == 0, LATS - 1, 0)
        base = slot * 4
        for q in range(4):
            landed(in_f, rf, base + q)
        tokens = load_blocks(in_f, base, 4)
        proj[...] = dot(tokens, qkv_w[...]).astype(BF)
        allowed = group_ids(iota((144, 1), 0), slot, edge) == group_ids(iota((1, 144), 1), slot, edge)
        allowed = jnp.concatenate([allowed, allowed], 0)
        for g in range(4):
            lanes = slice(128 * g, 128 * g + 128)
            query = halves(proj[:, lanes])
            key = proj[:, 512 + 128 * g : 640 + 128 * g]
            value = proj[:, 1024 + 128 * g : 1152 + 128 * g]
            scores = jnp.where(allowed, dot(query, key, 1, 1) * 0.125, MASK_FILL)
            lifted = jnp.exp(scores - jnp.max(scores, -1, keepdims=True))
            attend = lifted * (1.0 / jnp.sum(lifted, -1, keepdims=True))
            att[g] = attend
            ctx[:, lanes] = merge(dot(attend.astype(BF), value)).astype(BF)
        store_blocks(res_b, base, dot(ctx[...], out_w[...]).astype(BF), 4)
        send_back(slot, res_b, ret_b, sb, rb)

        for q in range(4):
            landed(in_c, rc, base + q)
        cot = load_blocks(in_c, base, 4)
        term = dot(ctx[...], cot, 0, 0).reshape(8, 2, 32, D)

        @pl.when(i == 0)
        def _():
            acc[...] = term

        @pl.when(i == 1)
        def _():
            acc[...] = (acc[...] + term) * factor
            a_src[...] = acc[:, 1 - core].astype(BF)
            pltpu.make_async_remote_copy(
                src_ref=a_src, dst_ref=a_dst, send_sem=a_sem.at[0], recv_sem=a_sem.at[1],
                device_id=(zl * 2 + 1 - core, lon), device_id_type=MESH,
            ).start()

        grad_ctx = dot(cot, out_w[...], 1, 1).astype(BF)
        for g in range(4):
            lanes = slice(128 * g, 128 * g + 128)
            query = halves(proj[:, lanes])
            key = proj[:, 512 + 128 * g : 640 + 128 * g]
            value = proj[:, 1024 + 128 * g : 1152 + 128 * g]
            grad_out = halves(grad_ctx[:, lanes])
            attend = att[g]
            grad_att = dot(grad_out, value, 1, 1)
            total = jnp.sum(attend * grad_att, -1, keepdims=True)
            grad_scores = (attend * (grad_att - total) * 0.125).astype(BF)
            gproj[:, lanes] = merge(dot(grad_scores, key)).astype(BF)
            gproj[:, 512 + 128 * g : 640 + 128 * g] = dot(grad_scores, query, 0, 0).astype(BF)
            gproj[:, 1024 + 128 * g : 1152 + 128 * g] = dot(attend.astype(BF), grad_out, 0, 0).astype(BF)
        store_blocks(res_g, base, dot(gproj[...], qkv_w[...], 1, 1).astype(BF), 4)
        send_back(slot, res_g, ret_g, sg, rg)
        return carry

    lax.fori_loop(0, 2, window, 0)

    a_copy = pltpu.make_async_remote_copy(
        src_ref=a_src, dst_ref=a_dst, send_sem=a_sem.at[0], recv_sem=a_sem.at[1],
        device_id=(zl * 2 + 1 - core, lon), device_id_type=MESH,
    )
    a_copy.wait()
    for x_ in range(4):
        both = acc[2 * x_ : 2 * x_ + 2, core] + a_dst[2 * x_ : 2 * x_ + 2].astype(F32)
        both = both.astype(BF).reshape(64, D)
        for y_ in range(4):
            b_src[y_ * 4 + x_] = both[:, 128 * y_ : 128 * y_ + 128]

    def b_copy(d):
        partner = yx ^ d
        return pltpu.make_async_remote_copy(
            src_ref=b_src.at[partner], dst_ref=b_dst.at[yx], send_sem=bs_sem.at[partner], recv_sem=br_sem.at[yx],
            device_id=at(partner // 4, partner % 4, z, core), device_id_type=MESH,
        )

    def b_start(d, carry):
        b_copy(d).start()
        return carry

    lax.fori_loop(1, 16, b_start, 0)
    b_dst[yx] = b_src[yx]

    def b_wait(d, carry):
        partner = yx ^ d
        pltpu.make_async_copy(b_dst.at[partner], b_dst.at[partner], br_sem.at[partner]).wait()
        pltpu.make_async_copy(b_src.at[partner], b_src.at[partner], bs_sem.at[partner]).wait()
        return carry

    lax.fori_loop(1, 16, b_wait, 0)
    c_src[...] = jnp.sum(b_dst[...].astype(F32), 0).reshape(2, 32, 128)

    for t in range(4):
        z_ = (t // 2) * 8 + 2 * x + t % 2

        @pl.when(z_ != z)
        def _():
            pltpu.make_async_remote_copy(
                src_ref=c_src.at[t % 2], dst_ref=c_dst.at[z], send_sem=cs_sem.at[t], recv_sem=cr_sem.at[z],
                device_id=at(y, x, z_, core), device_id_type=MESH,
            ).start()

    @pl.when(collector)
    def _():
        c_dst[z] = c_src[zl % 2]

        def c_wait(d, carry):
            partner = z ^ d
            pltpu.make_async_copy(c_dst.at[partner], c_dst.at[partner], cr_sem.at[partner]).wait()
            return carry

        lax.fori_loop(1, 16, c_wait, 0)
        d_src[...] = jnp.sum(c_dst[...], 0)
        for d in range(1, 4):
            pltpu.make_async_remote_copy(
                src_ref=d_src, dst_ref=d_dst, send_sem=ds_sem.at[d], recv_sem=dr_sem,
                device_id=at(y, x ^ d, z, core), device_id_type=MESH,
            ).start()

    for k in range(8):
        landed(ret_b, rb, k)
        landed(ret_g, rg, k)
    from_blocks = ones_where(grid_row(iota((1, 288), 1)) == iota((384, 288), 0))
    branch = dot(from_blocks, load_blocks(ret_b, 0, 8))
    wide = pad[0].reshape(384, D).astype(F32)
    layer_ref[...] = (wide + branch).astype(BF).reshape(24, 16, D)[:, 0:12]
    grad = dot(from_blocks, load_blocks(ret_g, 0, 8))
    normed_hat = hat[...]
    centred = grad - jnp.mean(grad, -1, keepdims=True)
    back = inv[...] * (centred - normed_hat * jnp.mean(grad * normed_hat, -1, keepdims=True))
    wide = pad[1].reshape(384, D).astype(F32)
    grad_ref[...] = (wide + back).astype(BF).reshape(24, 16, D)[:, 0:12]

    @pl.when(jnp.logical_not(collector))
    def _():
        pltpu.make_async_copy(d_dst, d_dst, dr_sem).wait()

    block = jnp.where(collector, d_src[...], d_dst[...])
    dw_ref[...] = pltpu.roll(block, (128 - 16 * (h * 4 + x)) % 128, 1)[:, 0:16]

    for k, (hlat, hlon, _) in enumerate(hosts):
        sent(out_f, sf, k, hlat, hlon)
        sent(out_c, sc, k, hlat, hlon)
    for i, (slat, slon, _) in enumerate(sources):
        sent(res_b, sb, i, slat, slon)
        sent(res_g, sg, i, slat, slon)
    for t in range(4):
        z_ = (t // 2) * 8 + 2 * x + t % 2

        @pl.when(z_ != z)
        def _():
            pltpu.make_async_copy(c_src.at[t % 2], c_src.at[t % 2], cs_sem.at[t]).wait()

    @pl.when(collector)
    def _():
        for d in range(1, 4):
            pltpu.make_async_copy(d_src, d_src, ds_sem.at[d]).wait()


def on_device(fields, qkv_weight, out_weight, cotangent):
    grid_shape = fields.shape
    tokens = fields.size // D * lax.axis_size("lat") * lax.axis_size("lon")
    factor = 1.0 / math.sqrt(tokens)
    vmem = pl.BlockSpec(memory_space=pltpu.VMEM)
    hbm = pl.BlockSpec(memory_space=pl.ANY)
    dma = pltpu.SemaphoreType.DMA
    layer, grad, dw = pl.pallas_call(
        functools.partial(kernel, factor),
        out_shape=[
            jax.ShapeDtypeStruct((24, 12, D), BF),
            jax.ShapeDtypeStruct((24, 12, D), BF),
            jax.ShapeDtypeStruct((32, 16), F32),
        ],
        in_specs=[vmem, hbm, hbm, vmem],
        out_specs=[vmem, vmem, vmem],
        scratch_shapes=[
            pltpu.VMEM((2, 24, 16, D), BF),
            pltpu.VMEM((384, D), F32),
            pltpu.VMEM((384, 1), F32),
            pltpu.VMEM((D, 3 * D), BF),
            pltpu.VMEM((D, D), BF),
        ]
        + [pltpu.VMEM((8,) + BLOCK, BF)] * 8
        + [
            pltpu.VMEM((144, 3 * D), BF),
            pltpu.VMEM((4, 288, 144), F32),
            pltpu.VMEM((144, D), BF),
            pltpu.VMEM((144, 3 * D), BF),
            pltpu.VMEM((8, 2, 32, D), F32),
            pltpu.VMEM((8, 32, D), BF),
            pltpu.VMEM((8, 32, D), BF),
            pltpu.VMEM((16, 64, 128), BF),
            pltpu.VMEM((16, 64, 128), BF),
            pltpu.VMEM((2, 32, 128), F32),
            pltpu.VMEM((16, 32, 128), F32),
            pltpu.VMEM((32, 128), F32),
            pltpu.VMEM((32, 128), F32),
            dma((2,)),
        ]
        + [dma((8,))] * 8
        + [dma((2,)), dma((16,)), dma((16,)), dma((4,)), dma((16,)), dma((4,)), dma],
        compiler_params=pltpu.CompilerParams(
            collective_id=0, has_side_effects=True, vmem_limit_bytes=48 * 2**20
        ),
        cost_estimate=pl.CostEstimate(flops=1_600_000_000, bytes_accessed=4_000_000, transcendentals=400_000),
        name="window_attention",
    )(fields.reshape(24, 12, D), qkv_weight, out_weight, cotangent.reshape(24, 12, D))
    return layer.reshape(grid_shape), grad.reshape(grid_shape), dw


def solution(mesh):
    in_specs = (P(None, "lat", "lon", None), P(), P(), P(None, "lat", "lon", None))
    out_specs = (P(None, "lat", "lon", None), P(None, "lat", "lon", None), P("lat", "lon"))
    return jax.shard_map(
        on_device, mesh=mesh, in_specs=in_specs, out_specs=out_specs, check_vma=False
    )
```

```python
import functools
import math

import jax
import jax.numpy as jnp
from jax import lax
from jax.experimental import pallas as pl
from jax.experimental.pallas import tpu as pltpu
from jax.sharding import PartitionSpec as P

MESH = pl.DeviceIdType.MESH
EPSILON = 1e-05
MASK_FILL = -1e30
BF = jnp.bfloat16
F32 = jnp.float32
D = 512
LATS = 16
LONS = 32
VMEM_LIMIT = 60 * 2**20
BLOCK = (16, 1152)


def dot(a, b, ca=1, cb=0):
    return lax.dot_general(a, b, (((ca,), (cb,)), ((), ())), preferred_element_type=F32)


def iota(shape, dim):
    return lax.broadcasted_iota(jnp.int32, shape, dim)


def ones_where(cond):
    return jnp.where(cond, 1.0, 0.0).astype(BF)


def z_quarter(lat, lon, back):
    zl = lat // 2
    h = (lon // 4) % 2
    low = (zl + 4) % 8
    wraps = 1 - zl // 4 if back else zl // 4
    return low * 2 + lat % 2, lon + ((h + wraps) % 2 - h) * 4


def moved(lat, lon, cond, back):
    qlat, qlon = z_quarter(lat, lon, back)
    return jnp.where(cond, qlat, lat), jnp.where(cond, qlon, lon)


def window_host(va, vb, slot):
    x = vb % 4
    odd = va % 2
    crossing = x == (3 if slot == 0 else 0)
    inner = x == (2 if slot == 0 else 1)
    step = 1 - 2 * slot
    hlat, hlon = moved(va, vb, crossing, False)
    shift = jnp.where(crossing, -step, jnp.where(inner, step, 0)) * odd
    return hlat, hlon + shift


def window_of(lat, lon, slot):
    x = lon % 4
    odd = lat % 2
    crossing = x == (3 - odd if slot == 0 else odd)
    inner = jnp.logical_and(x == (3 if slot == 0 else 0), odd == 1)
    step = 1 - 2 * slot
    vlat, vlon = moved(lat, lon, crossing, True)
    shift = jnp.where(crossing, step, jnp.where(inner, -step, 0)) * odd
    return vlat, vlon + shift


def block_host(lat, lon, r, c, p):
    kb = jnp.where(c == 1, lon, (lon + LONS - 1) % LONS)
    east = (kb + 1) % LONS
    q = (1 - r) * 2 + (1 - c)
    edge = lat == (LATS - 1 if r == 1 else 0)
    if p == 0:
        va = lat if r == 1 else jnp.where(edge, 0, lat - 1)
        slot1 = edge if r == 0 else None
        pos0, pos1 = q, 4 + q - 2
    else:
        va = lat if r == 0 else jnp.where(edge, lat, lat + 1)
        slot1 = None if r == 0 else jnp.logical_not(edge)
        pos0, pos1 = q + 2, 4 + q
    zero = window_host(va, kb, 0)
    one = window_host(va, east, 1)
    if slot1 is None:
        (hlat, hlon), pos = (zero, pos0) if p == 0 else (one, pos1)
    else:
        hlat, hlon = jnp.where(slot1, one[0], zero[0]), jnp.where(slot1, one[1], zero[1])
        pos = jnp.where(slot1, pos1, pos0)
    relayed = jnp.logical_and(kb % 4 == 3, va % 2 == 1)
    return hlat, hlon, pos, relayed


def inbox_source(lat, lon, slot, q):
    va, vb = window_of(lat, lon, slot)
    south, east = q // 2, q % 2
    if slot == 0:
        edge = va == LATS - 1
        if south == 0:
            slat, r, p = va, 1, 0
        else:
            slat = jnp.where(edge, va, va + 1)
            r = jnp.where(edge, 1, 0)
            p = jnp.where(edge, 1, 0)
        slon = (vb + east) % LONS
    else:
        edge = va == 0
        if south == 1:
            slat, r, p = va, 0, 1
        else:
            slat = jnp.where(edge, va, va - 1)
            r = jnp.where(edge, 0, 1)
            p = jnp.where(edge, 0, 1)
        slon = (vb + LONS - 1 + east) % LONS
    return slat, slon, (r * 2 + (1 - east)) * 2 + p


def grid_row(m):
    tail = m >= 256
    k = jnp.where(tail, (m - 256) >> 2, m >> 5)
    t = jnp.where(tail, 32 + ((m - 256) & 3), m & 31)
    r, c, p = k >> 2, (k >> 1) & 1, k & 1
    l2 = jnp.where(t >= 18, 1, 0)
    t = t - 18 * l2
    r3 = jnp.where(t >= 6, 1, 0) + jnp.where(t >= 12, 1, 0)
    lev = (1 + 2 * p + l2) & 3
    return ((3 * r + r3) * 12 + 6 * c + t - 6 * r3) * 4 + lev


def tail_map(count, j):
    rows = iota((4 * count, 1), 0)
    return ones_where((rows >> 2) * 16 + 4 * j + (rows & 3) == iota((4 * count, 16 * count), 1))


def store_blocks(ref, base, rows, count):
    for k in range(count):
        ref[base + k, :, 0:512] = rows[32 * k : 32 * k + 16]
        ref[base + k, :, 512:1024] = rows[32 * k + 16 : 32 * k + 32]
    tails = rows[32 * count :]
    packed = sum(
        dot(tail_map(count, j), tails[:, 128 * j : 128 * j + 128], 0, 0) for j in range(4)
    ).astype(BF)
    for k in range(count):
        ref[base + k, :, 1024:1152] = packed[16 * k : 16 * k + 16]


def load_blocks(ref, base, count):
    main = []
    for k in range(count):
        main += [ref[base + k, :, 0:512], ref[base + k, :, 512:1024]]
    packed = jnp.concatenate([ref[base + k, :, 1024:1152] for k in range(count)], 0)
    tails = jnp.concatenate([dot(tail_map(count, j), packed) for j in range(4)], 1).astype(BF)
    return jnp.concatenate(main + [tails], 0)


def group_ids(m, slot, edge):
    tail = m >= 128
    q = jnp.where(tail, (m - 128) >> 2, m >> 5)
    t = jnp.where(tail, 32 + ((m - 128) & 3), m & 31)
    l2 = jnp.where(t >= 18, 1, 0)
    south = q >> 1
    first = jnp.where(edge, south * (1 + l2), 0)
    second = jnp.where(edge, jnp.where(south == 0, 2, l2), l2)
    return jnp.where(slot == 0, first, second)


def kernel(
    factor,
    fields_hbm, qkv_hbm, out_hbm, cot_hbm,
    layer_ref, grad_ref, dw_ref,
    raw, wide_f, wide_c, hat, inv, dw_t, qkv_w, out_w,
    out_f, out_c, in_f, in_c, res_b, res_g, ret_b, ret_g, rel_f, rel_c,
    proj, att, ctx, gproj, acc,
    a_src, a_dst, b_src, b_dst, c_src, c_dst, d_src, d_dst,
    w_sem, sf, sc, sb, sg, rf, rc, rb, rg, tf, tc, uf, uc,
    a_sem, bs_sem, br_sem, cs_sem, cr_sem, ds_sem, dr_sem,
):
    lat = lax.axis_index("lat")
    lon = lax.axis_index("lon")
    core, zl = lat % 2, lat // 2
    y, h, x = lon // 8, (lon // 4) % 2, lon % 4
    z = h * 8 + zl
    yx = y * 4 + x
    collector = zl // 2 == x

    def at(y_, x_, z_, c_):
        return ((z_ % 8) * 2 + c_, y_ * 8 + (z_ // 8) * 4 + x_)

    def same(dlat, dlon):
        return jnp.logical_and(dlat == lat, dlon == lon)

    load_x = [
        pltpu.make_async_copy(fields_hbm, raw.at[0], w_sem.at[0]),
        pltpu.make_async_copy(cot_hbm, raw.at[1], w_sem.at[1]),
    ]
    load_w = [
        pltpu.make_async_copy(qkv_hbm, qkv_w, w_sem.at[2]),
        pltpu.make_async_copy(out_hbm, out_w, w_sem.at[3]),
    ]
    for copy in load_x + load_w:
        copy.start()

    far = jnp.where(x >= 2, 1, 0)
    hosts = []
    for j in range(8):
        r, p, c = (j >> 1) & 1, j & 1, far if j < 4 else 1 - far
        hosts.append(((r * 2 + c) * 2 + p,) + block_host(lat, lon, r, c, p))
    sources = [inbox_source(lat, lon, i // 4, i % 4) for i in range(8)]
    outer = lon + 2 * far - 1
    inner = lon + 1 - 2 * far
    relays = jnp.logical_or(x == 1, x == 2)
    passed = []
    for j in range(4):
        hlat, hlon, pos, relayed = block_host(lat, jnp.where(relays, outer, lon), (j >> 1) & 1, far, j & 1)
        passed.append((jnp.logical_and(relays, relayed), hlat, hlon, pos))

    barrier = pltpu.get_barrier_semaphore()

    def tell(dlat, dlon):
        pl.semaphore_signal(barrier, inc=1, device_id=(dlat, dlon), device_id_type=MESH)

    due = jnp.int32(16)
    for slat, slon, k in sources:
        cross = (jnp.where((k & 2) != 0, slon, slon + LONS - 1) % 4) == 3
        by = jnp.logical_and(cross, lat % 2 == 1)
        slon = slon + jnp.where(by, jnp.where(slon % 4 == 3, -1, 1), 0)
        pl.when(jnp.logical_not(same(slat, slon)))(functools.partial(tell, slat, slon))
    for j, (_, hlat, hlon, _, relayed) in enumerate(hosts):
        due = due + jnp.where(same(hlat, hlon), 0, 1)
    for flag, *_ in passed:
        due = due + jnp.where(flag, 1, 0)
        pl.when(flag)(functools.partial(tell, lat, outer))
    tell(zl * 2 + 1 - core, lon)

    def tell_plane(d, carry):
        partner = yx ^ d
        tell(*at(partner // 4, partner % 4, z, core))
        return carry

    lax.fori_loop(1, 16, tell_plane, 0)

    @pl.when(collector)
    def _():
        def tell_ring(d, carry):
            tell(*at(y, x, z ^ d, core))
            return carry

        lax.fori_loop(1, 16, tell_ring, 0)

    due = due + jnp.where(collector, 3, 4)

    to_blocks = ones_where(grid_row(iota((288, 1), 0)) == iota((288, 288), 1))
    load_x[0].wait()
    for i in range(72):
        wide_f[4 * i : 4 * i + 4] = raw[0, i].astype(F32)
    wide = wide_f[...]
    centred = wide - jnp.mean(wide, -1, keepdims=True)
    inverse = lax.rsqrt(jnp.mean(centred * centred, -1, keepdims=True) + EPSILON)
    normed_hat = centred * inverse
    hat[...] = normed_hat
    inv[...] = inverse
    store_blocks(out_f, 0, dot(to_blocks, normed_hat.astype(BF)).astype(BF), 8)
    load_x[1].wait()
    for i in range(72):
        wide_c[4 * i : 4 * i + 4] = raw[1, i].astype(F32)
    store_blocks(out_c, 0, dot(to_blocks, wide_c[...].astype(BF)).astype(BF), 8)

    pl.semaphore_wait(barrier, due)

    def send(src, dst, send_sems, recv_sems, i, dlat, dlon, j):
        here = same(dlat, dlon)

        @pl.when(here)
        def _():
            pltpu.make_async_copy(src.at[i], dst.at[j], recv_sems.at[j]).start()

        @pl.when(jnp.logical_not(here))
        def _():
            pltpu.make_async_remote_copy(
                src_ref=src.at[i], dst_ref=dst.at[j], send_sem=send_sems.at[i], recv_sem=recv_sems.at[j],
                device_id=(dlat, dlon), device_id_type=MESH,
            ).start()

    def landed(dst, sems, j):
        pltpu.make_async_copy(dst.at[j], dst.at[j], sems.at[j]).wait()

    def sent(src, sems, i, dlat, dlon):
        @pl.when(jnp.logical_not(same(dlat, dlon)))
        def _():
            pltpu.make_async_copy(src.at[i], src.at[i], sems.at[i]).wait()

    def relay_copy(src, dst, send_sems, recv_sems, k, j):
        return pltpu.make_async_remote_copy(
            src_ref=src.at[k], dst_ref=dst.at[j], send_sem=send_sems.at[k], recv_sem=recv_sems.at[j],
            device_id=(lat, inner), device_id_type=MESH,
        )

    halo = ((out_f, in_f, rel_f, sf, rf, tf, uf), (out_c, in_c, rel_c, sc, rc, tc, uc))
    for src, dst, rel, ss, rs, ts, us in halo:
        for j, (k, hlat, hlon, pos, relayed) in enumerate(hosts):
            if j < 4:
                pl.when(relayed)(lambda: relay_copy(src, rel, ss, ts, k, j).start())
                pl.when(jnp.logical_not(relayed))(lambda: send(src, dst, ss, rs, k, hlat, hlon, pos))
            else:
                send(src, dst, ss, rs, k, hlat, hlon, pos)
    for src, dst, rel, ss, rs, ts, us in halo:
        for j, (flag, hlat, hlon, pos) in enumerate(passed):
            @pl.when(flag)
            def _():
                landed(rel, ts, j)
                pltpu.make_async_remote_copy(
                    src_ref=rel.at[j], dst_ref=dst.at[pos], send_sem=us.at[j], recv_sem=rs.at[pos],
                    device_id=(hlat, hlon), device_id_type=MESH,
                ).start()

    for copy in load_w:
        copy.wait()

    first_half = iota((144, 128), 1) < 64

    def halves(pair):
        zero = jnp.zeros_like(pair)
        return jnp.concatenate([jnp.where(first_half, pair, zero), jnp.where(first_half, zero, pair)], 0)

    def merge(stacked):
        return jnp.where(first_half, stacked[:144], stacked[144:])

    def send_back(slot, src, dst, ss, rs):
        for s in range(2):
            @pl.when(slot == s)
            def _():
                for q in range(4):
                    slat, slon, k = sources[s * 4 + q]
                    send(src, dst, ss, rs, s * 4 + q, slat, slon, k)

    def a_copy():
        return pltpu.make_async_remote_copy(
            src_ref=a_src, dst_ref=a_dst, send_sem=a_sem.at[0], recv_sem=a_sem.at[1],
            device_id=(zl * 2 + 1 - core, lon), device_id_type=MESH,
        )

    def core_to_plane():
        a_copy().wait()
        for x_ in range(4):
            both = acc[2 * x_ : 2 * x_ + 2, core] + a_dst[2 * x_ : 2 * x_ + 2].astype(F32)
            both = both.astype(BF).reshape(64, D)
            for y_ in range(4):
                b_src[y_ * 4 + x_] = both[:, 128 * y_ : 128 * y_ + 128]

        def start(d, carry):
            partner = yx ^ d
            pltpu.make_async_remote_copy(
                src_ref=b_src.at[partner], dst_ref=b_dst.at[yx], send_sem=bs_sem.at[partner], recv_sem=br_sem.at[yx],
                device_id=at(partner // 4, partner % 4, z, core), device_id_type=MESH,
            ).start()
            return carry

        lax.fori_loop(1, 16, start, 0)
        b_dst[yx] = b_src[yx]

    def plane_to_ring():
        def wait(d, carry):
            partner = yx ^ d
            pltpu.make_async_copy(b_dst.at[partner], b_dst.at[partner], br_sem.at[partner]).wait()
            pltpu.make_async_copy(b_src.at[partner], b_src.at[partner], bs_sem.at[partner]).wait()
            return carry

        lax.fori_loop(1, 16, wait, 0)
        c_src[...] = jnp.sum(b_dst[...].astype(F32), 0).reshape(2, 32, 128)
        for t in range(4):
            z_ = (t // 2) * 8 + 2 * x + t % 2

            @pl.when(z_ != z)
            def _():
                pltpu.make_async_remote_copy(
                    src_ref=c_src.at[t % 2], dst_ref=c_dst.at[z], send_sem=cs_sem.at[t], recv_sem=cr_sem.at[z],
                    device_id=at(y, x, z_, core), device_id_type=MESH,
                ).start()

    edges = [window_of(lat, lon, 0)[0] == LATS - 1, window_of(lat, lon, 1)[0] == 0]

    def window(i, carry):
        slot = jnp.where(x == 3 - core, 1 - i, i)
        edge = jnp.where(slot == 0, edges[0], edges[1])
        base = slot * 4
        for q in range(4):
            landed(in_f, rf, base + q)
        tokens = load_blocks(in_f, base, 4)
        proj[...] = dot(tokens, qkv_w[...]).astype(BF)
        allowed = group_ids(iota((144, 1), 0), slot, edge) == group_ids(iota((1, 144), 1), slot, edge)
        allowed = jnp.concatenate([allowed, allowed], 0)
        for g in range(4):
            lanes = slice(128 * g, 128 * g + 128)
            query = halves(proj[:, lanes])
            key = proj[:, 512 + 128 * g : 640 + 128 * g]
            value = proj[:, 1024 + 128 * g : 1152 + 128 * g]
            scores = jnp.where(allowed, dot(query, key, 1, 1) * 0.125, MASK_FILL)
            lifted = jnp.exp(scores - jnp.max(scores, -1, keepdims=True))
            attend = lifted * (1.0 / jnp.sum(lifted, -1, keepdims=True))
            att[g] = attend
            ctx[:, lanes] = merge(dot(attend.astype(BF), value)).astype(BF)
        store_blocks(res_b, base, dot(ctx[...], out_w[...]).astype(BF), 4)
        send_back(slot, res_b, ret_b, sb, rb)

        for q in range(4):
            landed(in_c, rc, base + q)
        cot = load_blocks(in_c, base, 4)
        term = dot(ctx[...], cot, 0, 0).reshape(8, 2, 32, D)

        @pl.when(i == 0)
        def _():
            acc[...] = term

        @pl.when(i == 1)
        def _():
            acc[...] = (acc[...] + term) * factor
            a_src[...] = acc[:, 1 - core].astype(BF)
            a_copy().start()

        grad_ctx = dot(cot, out_w[...], 1, 1).astype(BF)
        for g in range(4):
            if g == 2:
                pl.when(i == 1)(core_to_plane)
            lanes = slice(128 * g, 128 * g + 128)
            query = halves(proj[:, lanes])
            key = proj[:, 512 + 128 * g : 640 + 128 * g]
            value = proj[:, 1024 + 128 * g : 1152 + 128 * g]
            grad_out = halves(grad_ctx[:, lanes])
            attend = att[g]
            grad_att = dot(grad_out, value, 1, 1)
            total = jnp.sum(attend * grad_att, -1, keepdims=True)
            grad_scores = (attend * (grad_att - total) * 0.125).astype(BF)
            gproj[:, lanes] = merge(dot(grad_scores, key)).astype(BF)
            gproj[:, 512 + 128 * g : 640 + 128 * g] = dot(grad_scores, query, 0, 0).astype(BF)
            gproj[:, 1024 + 128 * g : 1152 + 128 * g] = dot(attend.astype(BF), grad_out, 0, 0).astype(BF)
        store_blocks(res_g, base, dot(gproj[...], qkv_w[...], 1, 1).astype(BF), 4)
        send_back(slot, res_g, ret_g, sg, rg)
        pl.when(i == 1)(plane_to_ring)
        return carry

    lax.fori_loop(0, 2, window, 0)

    @pl.when(collector)
    def _():
        c_dst[z] = c_src[zl % 2]

        def c_wait(d, carry):
            partner = z ^ d
            pltpu.make_async_copy(c_dst.at[partner], c_dst.at[partner], cr_sem.at[partner]).wait()
            return carry

        lax.fori_loop(1, 16, c_wait, 0)
        d_src[...] = jnp.sum(c_dst[...], 0)
        for d in range(1, 4):
            pltpu.make_async_remote_copy(
                src_ref=d_src, dst_ref=d_dst, send_sem=ds_sem.at[d], recv_sem=dr_sem,
                device_id=at(y, x ^ d, z, core), device_id_type=MESH,
            ).start()

    for k in range(8):
        landed(ret_b, rb, k)
    from_blocks = ones_where(grid_row(iota((1, 288), 1)) == iota((288, 288), 0))
    wide_f[...] += dot(from_blocks, load_blocks(ret_b, 0, 8))
    for i in range(72):
        layer_ref[i] = wide_f[4 * i : 4 * i + 4].astype(BF)
    for k in range(8):
        landed(ret_g, rg, k)
    grad = dot(from_blocks, load_blocks(ret_g, 0, 8))
    normed_hat = hat[...]
    centred = grad - jnp.mean(grad, -1, keepdims=True)
    wide_c[...] += inv[...] * (centred - normed_hat * jnp.mean(grad * normed_hat, -1, keepdims=True))
    for i in range(72):
        grad_ref[i] = wide_c[4 * i : 4 * i + 4].astype(BF)

    @pl.when(jnp.logical_not(collector))
    def _():
        pltpu.make_async_copy(d_dst, d_dst, dr_sem).wait()

    dw_t[...] = jnp.where(collector, d_src[...], d_dst[...]).T
    dw_ref[...] = dw_t[pl.ds(pl.multiple_of(16 * (h * 4 + x), 16), 16)]

    for src, dst, rel, ss, rs, ts, us in halo:
        for k, hlat, hlon, _, _ in hosts:
            sent(src, ss, k, hlat, hlon)
        for j, (flag, *_) in enumerate(passed):
            pl.when(flag)(lambda: pltpu.make_async_copy(rel.at[j], rel.at[j], us.at[j]).wait())
    for i, (slat, slon, _) in enumerate(sources):
        sent(res_b, sb, i, slat, slon)
        sent(res_g, sg, i, slat, slon)
    for t in range(4):
        z_ = (t // 2) * 8 + 2 * x + t % 2

        @pl.when(z_ != z)
        def _():
            pltpu.make_async_copy(c_src.at[t % 2], c_src.at[t % 2], cs_sem.at[t]).wait()

    @pl.when(collector)
    def _():
        for d in range(1, 4):
            pltpu.make_async_copy(d_src, d_src, ds_sem.at[d]).wait()


def on_device(fields, qkv_weight, out_weight, cotangent):
    grid_shape = fields.shape
    tokens = fields.size // D * lax.axis_size("lat") * lax.axis_size("lon")
    factor = 1.0 / math.sqrt(tokens)
    vmem = pl.BlockSpec(memory_space=pltpu.VMEM)
    hbm = pl.BlockSpec(memory_space=pltpu.HBM)
    dma = pltpu.SemaphoreType.DMA
    layer, grad, dw = pl.pallas_call(
        functools.partial(kernel, factor),
        out_shape=[
            jax.ShapeDtypeStruct((72, 4, D), BF),
            jax.ShapeDtypeStruct((72, 4, D), BF),
            jax.ShapeDtypeStruct((16, 32), F32),
        ],
        in_specs=[hbm, hbm, hbm, hbm],
        out_specs=[vmem, vmem, vmem],
        scratch_shapes=[
            pltpu.VMEM((2, 72, 4, D), BF),
            pltpu.VMEM((288, D), F32),
            pltpu.VMEM((288, D), F32),
            pltpu.VMEM((288, D), F32),
            pltpu.VMEM((288, 1), F32),
            pltpu.VMEM((128, 32), F32),
            pltpu.VMEM((D, 3 * D), BF),
            pltpu.VMEM((D, D), BF),
        ]
        + [pltpu.VMEM((8,) + BLOCK, BF)] * 8
        + [pltpu.VMEM((4,) + BLOCK, BF)] * 2
        + [
            pltpu.VMEM((144, 3 * D), BF),
            pltpu.VMEM((4, 288, 144), F32),
            pltpu.VMEM((144, D), BF),
            pltpu.VMEM((144, 3 * D), BF),
            pltpu.VMEM((8, 2, 32, D), F32),
            pltpu.VMEM((8, 32, D), BF),
            pltpu.VMEM((8, 32, D), BF),
            pltpu.VMEM((16, 64, 128), BF),
            pltpu.VMEM((16, 64, 128), BF),
            pltpu.VMEM((2, 32, 128), F32),
            pltpu.VMEM((16, 32, 128), F32),
            pltpu.VMEM((32, 128), F32),
            pltpu.VMEM((32, 128), F32),
            dma((4,)),
        ]
        + [dma((8,))] * 8
        + [dma((4,))] * 4
        + [dma((2,)), dma((16,)), dma((16,)), dma((4,)), dma((16,)), dma((4,)), dma],
        compiler_params=pltpu.CompilerParams(
            collective_id=0, has_side_effects=True, vmem_limit_bytes=VMEM_LIMIT
        ),
        cost_estimate=pl.CostEstimate(flops=1_600_000_000, bytes_accessed=4_000_000, transcendentals=400_000),
        name="window_attention",
    )(by_place(fields), qkv_weight, out_weight, by_place(cotangent))
    layer, grad, dw = hand_out(layer, grad, dw)
    return from_place(layer, grid_shape), from_place(grad, grid_shape), dw.T


def hand_out(*arrays):
    count = len(arrays)

    def kernel(*refs):
        for i in range(count):
            refs[count + i][...] = refs[i][...]

    return pl.pallas_call(
        kernel,
        out_shape=[jax.ShapeDtypeStruct(a.shape, a.dtype) for a in arrays],
        in_specs=[pl.BlockSpec(memory_space=pltpu.VMEM)] * count,
        out_specs=[pl.BlockSpec(memory_space=pltpu.VMEM)] * count,
        name="hand_out",
    )(*arrays)


def by_place(grid):
    return grid.transpose(1, 2, 0, 3).reshape(72, 4, D)


def from_place(tokens, grid_shape):
    lev, lat, lon, d = grid_shape
    return tokens.reshape(lat, lon, lev, d).transpose(2, 0, 1, 3)


def solution(mesh):
    in_specs = (P(None, "lat", "lon", None), P(), P(), P(None, "lat", "lon", None))
    out_specs = (P(None, "lat", "lon", None), P(None, "lat", "lon", None), P("lat", "lon"))
    return jax.shard_map(
        on_device, mesh=mesh, in_specs=in_specs, out_specs=out_specs, check_vma=False
    )
```

```python
import functools
import math

import jax
import jax.numpy as jnp
from jax import lax
from jax.experimental import pallas as pl
from jax.experimental.pallas import tpu as pltpu
from jax.sharding import PartitionSpec as P

MESH = pl.DeviceIdType.MESH
EPSILON = 1e-05
MASK_FILL = -1e30
BF = jnp.bfloat16
F32 = jnp.float32
D = 512
LATS = 16
LONS = 32
VMEM_LIMIT = 60 * 2**20
BLOCK = (16, 1152)


def dot(a, b, ca=1, cb=0):
    return lax.dot_general(a, b, (((ca,), (cb,)), ((), ())), preferred_element_type=F32)


def iota(shape, dim):
    return lax.broadcasted_iota(jnp.int32, shape, dim)


def ones_where(cond):
    return jnp.where(cond, 1.0, 0.0).astype(BF)


def z_quarter(lat, lon, back):
    zl = lat // 2
    h = (lon // 4) % 2
    low = (zl + 4) % 8
    wraps = 1 - zl // 4 if back else zl // 4
    return low * 2 + lat % 2, lon + ((h + wraps) % 2 - h) * 4


def moved(lat, lon, cond, back):
    qlat, qlon = z_quarter(lat, lon, back)
    return jnp.where(cond, qlat, lat), jnp.where(cond, qlon, lon)


def window_host(va, vb, slot):
    x = vb % 4
    odd = va % 2
    crossing = x == (3 if slot == 0 else 0)
    inner = x == (2 if slot == 0 else 1)
    step = 1 - 2 * slot
    hlat, hlon = moved(va, vb, crossing, False)
    shift = jnp.where(crossing, -step, jnp.where(inner, step, 0)) * odd
    return hlat, hlon + shift


def window_of(lat, lon, slot):
    x = lon % 4
    odd = lat % 2
    crossing = x == (3 - odd if slot == 0 else odd)
    inner = jnp.logical_and(x == (3 if slot == 0 else 0), odd == 1)
    step = 1 - 2 * slot
    vlat, vlon = moved(lat, lon, crossing, True)
    shift = jnp.where(crossing, step, jnp.where(inner, -step, 0)) * odd
    return vlat, vlon + shift


def block_host(lat, lon, r, c, p):
    kb = jnp.where(c == 1, lon, (lon + LONS - 1) % LONS)
    east = (kb + 1) % LONS
    q = (1 - r) * 2 + (1 - c)
    edge = lat == (LATS - 1 if r == 1 else 0)
    if p == 0:
        va = lat if r == 1 else jnp.where(edge, 0, lat - 1)
        slot1 = edge if r == 0 else None
        pos0, pos1 = q, 4 + q - 2
    else:
        va = lat if r == 0 else jnp.where(edge, lat, lat + 1)
        slot1 = None if r == 0 else jnp.logical_not(edge)
        pos0, pos1 = q + 2, 4 + q
    zero = window_host(va, kb, 0)
    one = window_host(va, east, 1)
    if slot1 is None:
        (hlat, hlon), pos = (zero, pos0) if p == 0 else (one, pos1)
    else:
        hlat, hlon = jnp.where(slot1, one[0], zero[0]), jnp.where(slot1, one[1], zero[1])
        pos = jnp.where(slot1, pos1, pos0)
    relayed = jnp.logical_and(kb % 4 == 3, va % 2 == 1)
    return hlat, hlon, pos, relayed


def inbox_source(lat, lon, slot, q):
    va, vb = window_of(lat, lon, slot)
    south, east = q // 2, q % 2
    if slot == 0:
        edge = va == LATS - 1
        if south == 0:
            slat, r, p = va, 1, 0
        else:
            slat = jnp.where(edge, va, va + 1)
            r = jnp.where(edge, 1, 0)
            p = jnp.where(edge, 1, 0)
        slon = (vb + east) % LONS
    else:
        edge = va == 0
        if south == 1:
            slat, r, p = va, 0, 1
        else:
            slat = jnp.where(edge, va, va - 1)
            r = jnp.where(edge, 0, 1)
            p = jnp.where(edge, 0, 1)
        slon = (vb + LONS - 1 + east) % LONS
    return slat, slon, (r * 2 + (1 - east)) * 2 + p


def grid_row(m):
    tail = m >= 256
    k = jnp.where(tail, (m - 256) >> 2, m >> 5)
    t = jnp.where(tail, 32 + ((m - 256) & 3), m & 31)
    r, c, p = k >> 2, (k >> 1) & 1, k & 1
    l2 = jnp.where(t >= 18, 1, 0)
    t = t - 18 * l2
    r3 = jnp.where(t >= 6, 1, 0) + jnp.where(t >= 12, 1, 0)
    lev = (1 + 2 * p + l2) & 3
    return ((3 * r + r3) * 12 + 6 * c + t - 6 * r3) * 4 + lev


def tail_map(count, j):
    rows = iota((4 * count, 1), 0)
    return ones_where((rows >> 2) * 16 + 4 * j + (rows & 3) == iota((4 * count, 16 * count), 1))


def store_blocks(ref, base, rows, count):
    for k in range(count):
        ref[base + k, :, 0:512] = rows[32 * k : 32 * k + 16]
        ref[base + k, :, 512:1024] = rows[32 * k + 16 : 32 * k + 32]
    tails = rows[32 * count :]
    packed = sum(
        dot(tail_map(count, j), tails[:, 128 * j : 128 * j + 128], 0, 0) for j in range(4)
    ).astype(BF)
    for k in range(count):
        ref[base + k, :, 1024:1152] = packed[16 * k : 16 * k + 16]


def load_blocks(ref, base, count):
    main = []
    for k in range(count):
        main += [ref[base + k, :, 0:512], ref[base + k, :, 512:1024]]
    packed = jnp.concatenate([ref[base + k, :, 1024:1152] for k in range(count)], 0)
    tails = jnp.concatenate([dot(tail_map(count, j), packed) for j in range(4)], 1).astype(BF)
    return jnp.concatenate(main + [tails], 0)


def group_ids(m, slot, edge):
    tail = m >= 128
    q = jnp.where(tail, (m - 128) >> 2, m >> 5)
    t = jnp.where(tail, 32 + ((m - 128) & 3), m & 31)
    l2 = jnp.where(t >= 18, 1, 0)
    south = q >> 1
    first = jnp.where(edge, south * (1 + l2), 0)
    second = jnp.where(edge, jnp.where(south == 0, 2, l2), l2)
    return jnp.where(slot == 0, first, second)


def kernel(
    factor,
    fields_hbm, qkv_hbm, out_hbm, cot_hbm,
    layer_ref, grad_ref, dw_ref,
    raw, wide_f, wide_c, hat, inv, dw_t, qkv_w, out_w,
    out_f, out_c, in_f, in_c, res_b, res_g, ret_b, ret_g, rel_f, rel_c,
    proj, att, ctx, cots, gctx, gproj, acc,
    a_src, a_dst, b_src, b_dst, c_src, c_dst, d_src, d_dst,
    w_sem, sf, sc, sb, sg, rf, rc, rb, rg, tf, tc, uf, uc,
    a_sem, bs_sem, br_sem, cs_sem, cr_sem, ds_sem, dr_sem, ring_sem,
):
    lat = lax.axis_index("lat")
    lon = lax.axis_index("lon")
    core, zl = lat % 2, lat // 2
    y, h, x = lon // 8, (lon // 4) % 2, lon % 4
    z = h * 8 + zl
    yx = y * 4 + x
    collector = zl // 2 == x

    def at(y_, x_, z_, c_):
        return ((z_ % 8) * 2 + c_, y_ * 8 + (z_ // 8) * 4 + x_)

    def same(dlat, dlon):
        return jnp.logical_and(dlat == lat, dlon == lon)

    load_x = [
        pltpu.make_async_copy(fields_hbm, raw.at[0], w_sem.at[0]),
        pltpu.make_async_copy(cot_hbm, raw.at[1], w_sem.at[1]),
    ]
    load_w = [
        pltpu.make_async_copy(qkv_hbm, qkv_w, w_sem.at[2]),
        pltpu.make_async_copy(out_hbm, out_w, w_sem.at[3]),
    ]
    for copy in load_x + load_w:
        copy.start()

    far = jnp.where(x >= 2, 1, 0)
    hosts = []
    for j in range(8):
        r, p, c = (j >> 1) & 1, j & 1, far if j < 4 else 1 - far
        hosts.append(((r * 2 + c) * 2 + p,) + block_host(lat, lon, r, c, p))
    sources = [inbox_source(lat, lon, i // 4, i % 4) for i in range(8)]
    outer = lon + 2 * far - 1
    inner = lon + 1 - 2 * far
    relays = jnp.logical_or(x == 1, x == 2)
    passed = []
    for j in range(4):
        hlat, hlon, pos, relayed = block_host(lat, jnp.where(relays, outer, lon), (j >> 1) & 1, far, j & 1)
        passed.append((jnp.logical_and(relays, relayed), hlat, hlon, pos))

    barrier = pltpu.get_barrier_semaphore()

    def tell(dlat, dlon):
        pl.semaphore_signal(barrier, inc=1, device_id=(dlat, dlon), device_id_type=MESH)

    due = jnp.int32(16)
    for slat, slon, k in sources:
        cross = (jnp.where((k & 2) != 0, slon, slon + LONS - 1) % 4) == 3
        by = jnp.logical_and(cross, lat % 2 == 1)
        slon = slon + jnp.where(by, jnp.where(slon % 4 == 3, -1, 1), 0)
        pl.when(jnp.logical_not(same(slat, slon)))(functools.partial(tell, slat, slon))
    for j, (_, hlat, hlon, _, relayed) in enumerate(hosts):
        due = due + jnp.where(same(hlat, hlon), 0, 1)
    for flag, *_ in passed:
        due = due + jnp.where(flag, 1, 0)
        pl.when(flag)(functools.partial(tell, lat, outer))
    for d in (4, 12):
        tell(*at(y, x, (z + d) % 16, core))

    @pl.when(collector)
    def _():
        for d in (3, 13, 2, 14, 1, 15):
            tell(*at(y, x, (z + d) % 16, core))

    for collecting in (0, 1, 8, 9):
        away = (2 * x + collecting - z + 16) % 16
        due = due + jnp.where((away >= 1) & (away <= 3) | (away >= 13), 1, 0)

    def tell_plane(d, carry):
        partner = yx ^ d
        tell(*at(partner // 4, partner % 4, z, core))
        return carry

    lax.fori_loop(1, 16, tell_plane, 0)
    tell(zl * 2 + 1 - core, lon)

    due = due + 2

    to_blocks = ones_where(grid_row(iota((288, 1), 0)) == iota((288, 288), 1))
    load_x[0].wait()
    for i in range(72):
        wide_f[4 * i : 4 * i + 4] = raw[0, i].astype(F32)
    wide = wide_f[...]
    centred = wide - jnp.mean(wide, -1, keepdims=True)
    inverse = lax.rsqrt(jnp.mean(centred * centred, -1, keepdims=True) + EPSILON)
    normed_hat = centred * inverse
    hat[...] = normed_hat
    inv[...] = inverse
    store_blocks(out_f, 0, dot(to_blocks, normed_hat.astype(BF)).astype(BF), 8)
    load_x[1].wait()
    for i in range(72):
        wide_c[4 * i : 4 * i + 4] = raw[1, i].astype(F32)
    store_blocks(out_c, 0, dot(to_blocks, wide_c[...].astype(BF)).astype(BF), 8)

    pl.semaphore_wait(barrier, due)
    for d in (4, 12):
        pl.semaphore_signal(
            ring_sem, inc=1, device_id=at(y, x, (z + d) % 16, core), device_id_type=MESH
        )

    def send(src, dst, send_sems, recv_sems, i, dlat, dlon, j):
        here = same(dlat, dlon)

        @pl.when(here)
        def _():
            pltpu.make_async_copy(src.at[i], dst.at[j], recv_sems.at[j]).start()

        @pl.when(jnp.logical_not(here))
        def _():
            pltpu.make_async_remote_copy(
                src_ref=src.at[i], dst_ref=dst.at[j], send_sem=send_sems.at[i], recv_sem=recv_sems.at[j],
                device_id=(dlat, dlon), device_id_type=MESH,
            ).start()

    def landed(dst, sems, j):
        pltpu.make_async_copy(dst.at[j], dst.at[j], sems.at[j]).wait()

    def sent(src, sems, i, dlat, dlon):
        @pl.when(jnp.logical_not(same(dlat, dlon)))
        def _():
            pltpu.make_async_copy(src.at[i], src.at[i], sems.at[i]).wait()

    def relay_copy(src, dst, send_sems, recv_sems, k, j):
        return pltpu.make_async_remote_copy(
            src_ref=src.at[k], dst_ref=dst.at[j], send_sem=send_sems.at[k], recv_sem=recv_sems.at[j],
            device_id=(lat, inner), device_id_type=MESH,
        )

    halo = ((out_f, in_f, rel_f, sf, rf, tf, uf), (out_c, in_c, rel_c, sc, rc, tc, uc))
    for src, dst, rel, ss, rs, ts, us in halo:
        for j, (k, hlat, hlon, pos, relayed) in enumerate(hosts[:4]):
            pl.when(relayed)(lambda: relay_copy(src, rel, ss, ts, k, j).start())
            pl.when(jnp.logical_not(relayed))(lambda: send(src, dst, ss, rs, k, hlat, hlon, pos))
    for src, dst, rel, ss, rs, ts, us in halo:
        for k, hlat, hlon, pos, _ in hosts[4:]:
            send(src, dst, ss, rs, k, hlat, hlon, pos)
    for src, dst, rel, ss, rs, ts, us in halo:
        for j, (flag, hlat, hlon, pos) in enumerate(passed):
            @pl.when(flag)
            def _():
                landed(rel, ts, j)
                pltpu.make_async_remote_copy(
                    src_ref=rel.at[j], dst_ref=dst.at[pos], send_sem=us.at[j], recv_sem=rs.at[pos],
                    device_id=(hlat, hlon), device_id_type=MESH,
                ).start()

    for copy in load_w:
        copy.wait()

    first_half = iota((144, 128), 1) < 64

    def halves(pair):
        zero = jnp.zeros_like(pair)
        return jnp.concatenate([jnp.where(first_half, pair, zero), jnp.where(first_half, zero, pair)], 0)

    def merge(stacked):
        return jnp.where(first_half, stacked[:144], stacked[144:])

    def send_back(slot, src, dst, ss, rs):
        def go(s):
            for q in range(4):
                slat, slon, k = sources[s * 4 + q]
                send(src, dst, ss, rs, s * 4 + q, slat, slon, k)

        if isinstance(slot, int):
            go(slot)
        else:
            for s in range(2):
                pl.when(slot == s)(functools.partial(go, s))

    def a_copy():
        return pltpu.make_async_remote_copy(
            src_ref=a_src, dst_ref=a_dst, send_sem=a_sem.at[0], recv_sem=a_sem.at[1],
            device_id=(zl * 2 + 1 - core, lon), device_id_type=MESH,
        )

    def core_to_plane():
        a_copy().wait()
        for x_ in range(4):
            both = acc[2 * x_ : 2 * x_ + 2, core] + a_dst[2 * x_ : 2 * x_ + 2].astype(F32)
            both = both.astype(BF).reshape(64, D)
            for y_ in range(4):
                b_src[y_ * 4 + x_] = both[:, 128 * y_ : 128 * y_ + 128]

        def start(d, carry):
            partner = yx ^ d
            pltpu.make_async_remote_copy(
                src_ref=b_src.at[partner], dst_ref=b_dst.at[yx], send_sem=bs_sem.at[partner], recv_sem=br_sem.at[yx],
                device_id=at(partner // 4, partner % 4, z, core), device_id_type=MESH,
            ).start()
            return carry

        lax.fori_loop(1, 16, start, 0)
        b_dst[yx] = b_src[yx]

    def plane_to_ring():
        def wait(d, carry):
            partner = yx ^ d
            pltpu.make_async_copy(b_dst.at[partner], b_dst.at[partner], br_sem.at[partner]).wait()
            pltpu.make_async_copy(b_src.at[partner], b_src.at[partner], bs_sem.at[partner]).wait()
            return carry

        lax.fori_loop(1, 16, wait, 0)
        c_src[...] = jnp.sum(b_dst[...].astype(F32), 0).astype(BF).reshape(2, 32, 128)
        pl.semaphore_wait(ring_sem, 2)
        for t in range(4):
            z_ = (t // 2) * 8 + 2 * x + t % 2

            @pl.when(z_ != z)
            def _():
                pltpu.make_async_remote_copy(
                    src_ref=c_src.at[t % 2], dst_ref=c_dst.at[z], send_sem=cs_sem.at[t], recv_sem=cr_sem.at[z],
                    device_id=at(y, x, z_, core), device_id_type=MESH,
                ).start()

    edges = [window_of(lat, lon, 0)[0] == LATS - 1, window_of(lat, lon, 1)[0] == 0]

    def slot_of(i):
        return jnp.where(x == 3 - core, 1 - i, i)

    def forward(i, carry):
        slot = slot_of(i)
        edge = jnp.where(slot == 0, edges[0], edges[1])
        for q in range(4):
            landed(in_f, rf, slot * 4 + q)
        proj[slot] = dot(load_blocks(in_f, slot * 4, 4), qkv_w[...]).astype(BF)
        allowed = group_ids(iota((144, 1), 0), slot, edge) == group_ids(iota((1, 144), 1), slot, edge)
        allowed = jnp.concatenate([allowed, allowed], 0)
        for g in range(4):
            lanes = slice(128 * g, 128 * g + 128)
            query = halves(proj[slot, :, lanes])
            key = proj[slot, :, 512 + 128 * g : 640 + 128 * g]
            value = proj[slot, :, 1024 + 128 * g : 1152 + 128 * g]
            scores = jnp.where(allowed, dot(query, key, 1, 1) * 0.125, MASK_FILL)
            lifted = jnp.exp(scores - jnp.max(scores, -1, keepdims=True))
            attend = lifted * (1.0 / jnp.sum(lifted, -1, keepdims=True))
            att[slot * 4 + g] = attend
            ctx[slot, :, lanes] = merge(dot(attend.astype(BF), value)).astype(BF)
        return carry

    lax.fori_loop(0, 2, forward, 0)

    for i in range(2):
        slot = slot_of(i)
        for q in range(4):
            landed(in_c, rc, slot * 4 + q)
        cots[slot] = load_blocks(in_c, slot * 4, 4)
    both_ctx = ctx[...].reshape(288, D)
    both_cot = cots[...].reshape(288, D)
    acc[...] = (dot(both_ctx, both_cot, 0, 0) * factor).reshape(8, 2, 32, D)
    a_src[...] = acc[:, 1 - core].astype(BF)
    a_copy().start()

    branch = dot(both_ctx, out_w[...]).astype(BF)
    for slot in range(2):
        store_blocks(res_b, slot * 4, branch[144 * slot : 144 * slot + 144], 4)
        send_back(slot, res_b, ret_b, sb, rb)
    gctx[...] = dot(both_cot, out_w[...], 1, 1).astype(BF).reshape(2, 144, D)
    core_to_plane()

    def backward(i, carry):
        slot = slot_of(i)
        for g in range(4):
            lanes = slice(128 * g, 128 * g + 128)
            query = halves(proj[slot, :, lanes])
            key = proj[slot, :, 512 + 128 * g : 640 + 128 * g]
            value = proj[slot, :, 1024 + 128 * g : 1152 + 128 * g]
            grad_out = halves(gctx[slot, :, lanes])
            attend = att[slot * 4 + g]
            grad_att = dot(grad_out, value, 1, 1)
            total = jnp.sum(attend * grad_att, -1, keepdims=True)
            grad_scores = (attend * (grad_att - total) * 0.125).astype(BF)
            gproj[:, lanes] = merge(dot(grad_scores, key)).astype(BF)
            gproj[:, 512 + 128 * g : 640 + 128 * g] = dot(grad_scores, query, 0, 0).astype(BF)
            gproj[:, 1024 + 128 * g : 1152 + 128 * g] = dot(attend.astype(BF), grad_out, 0, 0).astype(BF)
        store_blocks(res_g, slot * 4, dot(gproj[...], qkv_w[...], 1, 1).astype(BF), 4)
        send_back(slot, res_g, ret_g, sg, rg)
        return carry

    lax.fori_loop(0, 2, backward, 0)
    plane_to_ring()

    @pl.when(collector)
    def _():
        c_dst[z] = c_src[zl % 2]

        def c_wait(d, carry):
            partner = z ^ d
            pltpu.make_async_copy(c_dst.at[partner], c_dst.at[partner], cr_sem.at[partner]).wait()
            return carry

        lax.fori_loop(1, 16, c_wait, 0)
        d_src[...] = jnp.sum(c_dst[...].astype(F32), 0)
        for d in range(1, 4):
            pltpu.make_async_remote_copy(
                src_ref=d_src, dst_ref=d_dst, send_sem=ds_sem.at[d], recv_sem=dr_sem,
                device_id=at(y, x ^ d, z, core), device_id_type=MESH,
            ).start()

    for k in range(8):
        landed(ret_b, rb, k)
    from_blocks = ones_where(grid_row(iota((1, 288), 1)) == iota((288, 288), 0))
    wide_f[...] += dot(from_blocks, load_blocks(ret_b, 0, 8))
    for i in range(72):
        layer_ref[i] = wide_f[4 * i : 4 * i + 4].astype(BF)
    for k in range(8):
        landed(ret_g, rg, k)
    grad = dot(from_blocks, load_blocks(ret_g, 0, 8))
    normed_hat = hat[...]
    centred = grad - jnp.mean(grad, -1, keepdims=True)
    wide_c[...] += inv[...] * (centred - normed_hat * jnp.mean(grad * normed_hat, -1, keepdims=True))
    for i in range(72):
        grad_ref[i] = wide_c[4 * i : 4 * i + 4].astype(BF)

    @pl.when(jnp.logical_not(collector))
    def _():
        pltpu.make_async_copy(d_dst, d_dst, dr_sem).wait()

    dw_t[...] = jnp.where(collector, d_src[...], d_dst[...]).T
    dw_ref[...] = dw_t[pl.ds(pl.multiple_of(16 * (h * 4 + x), 16), 16)]

    for src, dst, rel, ss, rs, ts, us in halo:
        for k, hlat, hlon, _, _ in hosts:
            sent(src, ss, k, hlat, hlon)
        for j, (flag, *_) in enumerate(passed):
            pl.when(flag)(lambda: pltpu.make_async_copy(rel.at[j], rel.at[j], us.at[j]).wait())
    for i, (slat, slon, _) in enumerate(sources):
        sent(res_b, sb, i, slat, slon)
        sent(res_g, sg, i, slat, slon)
    for t in range(4):
        z_ = (t // 2) * 8 + 2 * x + t % 2

        @pl.when(z_ != z)
        def _():
            pltpu.make_async_copy(c_src.at[t % 2], c_src.at[t % 2], cs_sem.at[t]).wait()

    @pl.when(collector)
    def _():
        for d in range(1, 4):
            pltpu.make_async_copy(d_src, d_src, ds_sem.at[d]).wait()


def on_device(fields, qkv_weight, out_weight, cotangent):
    grid_shape = fields.shape
    tokens = fields.size // D * lax.axis_size("lat") * lax.axis_size("lon")
    factor = 1.0 / math.sqrt(tokens)
    vmem = pl.BlockSpec(memory_space=pltpu.VMEM)
    hbm = pl.BlockSpec(memory_space=pltpu.HBM)
    dma = pltpu.SemaphoreType.DMA
    layer, grad, dw = pl.pallas_call(
        functools.partial(kernel, factor),
        out_shape=[
            jax.ShapeDtypeStruct((72, 4, D), BF),
            jax.ShapeDtypeStruct((72, 4, D), BF),
            jax.ShapeDtypeStruct((16, 32), F32),
        ],
        in_specs=[hbm, hbm, hbm, hbm],
        out_specs=[vmem, vmem, vmem],
        scratch_shapes=[
            pltpu.VMEM((2, 72, 4, D), BF),
            pltpu.VMEM((288, D), F32),
            pltpu.VMEM((288, D), F32),
            pltpu.VMEM((288, D), F32),
            pltpu.VMEM((288, 1), F32),
            pltpu.VMEM((128, 32), F32),
            pltpu.VMEM((D, 3 * D), BF),
            pltpu.VMEM((D, D), BF),
        ]
        + [pltpu.VMEM((8,) + BLOCK, BF)] * 8
        + [pltpu.VMEM((4,) + BLOCK, BF)] * 2
        + [
            pltpu.VMEM((2, 144, 3 * D), BF),
            pltpu.VMEM((8, 288, 144), F32),
            pltpu.VMEM((2, 144, D), BF),
            pltpu.VMEM((2, 144, D), BF),
            pltpu.VMEM((2, 144, D), BF),
            pltpu.VMEM((144, 3 * D), BF),
            pltpu.VMEM((8, 2, 32, D), F32),
            pltpu.VMEM((8, 32, D), BF),
            pltpu.VMEM((8, 32, D), BF),
            pltpu.VMEM((16, 64, 128), BF),
            pltpu.VMEM((16, 64, 128), BF),
            pltpu.VMEM((2, 32, 128), BF),
            pltpu.VMEM((16, 32, 128), BF),
            pltpu.VMEM((32, 128), F32),
            pltpu.VMEM((32, 128), F32),
            dma((4,)),
        ]
        + [dma((8,))] * 8
        + [dma((4,))] * 4
        + [dma((2,)), dma((16,)), dma((16,)), dma((4,)), dma((16,)), dma((4,)), dma, pltpu.SemaphoreType.REGULAR],
        compiler_params=pltpu.CompilerParams(
            collective_id=0, has_side_effects=True, vmem_limit_bytes=VMEM_LIMIT
        ),
        cost_estimate=pl.CostEstimate(flops=1_600_000_000, bytes_accessed=4_000_000, transcendentals=400_000),
        name="window_attention",
    )(by_place(fields), qkv_weight, out_weight, by_place(cotangent))
    layer, grad, dw = hand_out(layer, grad, dw)
    return from_place(layer, grid_shape), from_place(grad, grid_shape), dw.T


def hand_out(*arrays):
    count = len(arrays)

    def kernel(*refs):
        for i in range(count):
            refs[count + i][...] = refs[i][...]

    return pl.pallas_call(
        kernel,
        out_shape=[jax.ShapeDtypeStruct(a.shape, a.dtype) for a in arrays],
        in_specs=[pl.BlockSpec(memory_space=pltpu.VMEM)] * count,
        out_specs=[pl.BlockSpec(memory_space=pltpu.VMEM)] * count,
        name="hand_out",
    )(*arrays)


def by_place(grid):
    return grid.transpose(1, 2, 0, 3).reshape(72, 4, D)


def from_place(tokens, grid_shape):
    lev, lat, lon, d = grid_shape
    return tokens.reshape(lat, lon, lev, d).transpose(2, 0, 1, 3)


def solution(mesh):
    in_specs = (P(None, "lat", "lon", None), P(), P(), P(None, "lat", "lon", None))
    out_specs = (P(None, "lat", "lon", None), P(None, "lat", "lon", None), P("lat", "lon"))
    return jax.shard_map(
        on_device, mesh=mesh, in_specs=in_specs, out_specs=out_specs, check_vma=False
    )
```

```python
import functools
import math

import jax
import jax.numpy as jnp
from jax import lax
from jax.experimental import pallas as pl
from jax.experimental.pallas import tpu as pltpu
from jax.sharding import PartitionSpec as P

MESH = pl.DeviceIdType.MESH
EPSILON = 1e-05
MASK_FILL = -1e30
BF = jnp.bfloat16
F32 = jnp.float32
D = 512
LATS = 16
LONS = 32
VMEM_LIMIT = 60 * 2**20
BLOCK = (16, 1152)
FAR_FIRST = (10, 9, 11, 6, 14, 8, 2, 5, 7, 13, 15, 4, 12, 1, 3)


def dot(a, b, ca=1, cb=0):
    return lax.dot_general(a, b, (((ca,), (cb,)), ((), ())), preferred_element_type=F32)


def iota(shape, dim):
    return lax.broadcasted_iota(jnp.int32, shape, dim)


def ones_where(cond):
    return jnp.where(cond, 1.0, 0.0).astype(BF)


def z_quarter(lat, lon, back):
    zl = lat // 2
    h = (lon // 4) % 2
    low = (zl + 4) % 8
    wraps = 1 - zl // 4 if back else zl // 4
    return low * 2 + lat % 2, lon + ((h + wraps) % 2 - h) * 4


def moved(lat, lon, cond, back):
    qlat, qlon = z_quarter(lat, lon, back)
    return jnp.where(cond, qlat, lat), jnp.where(cond, qlon, lon)


def window_host(va, vb, slot):
    x = vb % 4
    odd = va % 2
    crossing = x == (3 if slot == 0 else 0)
    inner = x == (2 if slot == 0 else 1)
    step = 1 - 2 * slot
    hlat, hlon = moved(va, vb, crossing, False)
    shift = jnp.where(crossing, -step, jnp.where(inner, step, 0)) * odd
    return hlat, hlon + shift


def window_of(lat, lon, slot):
    x = lon % 4
    odd = lat % 2
    crossing = x == (3 - odd if slot == 0 else odd)
    inner = jnp.logical_and(x == (3 if slot == 0 else 0), odd == 1)
    step = 1 - 2 * slot
    vlat, vlon = moved(lat, lon, crossing, True)
    shift = jnp.where(crossing, step, jnp.where(inner, -step, 0)) * odd
    return vlat, vlon + shift


def block_host(lat, lon, r, c, p):
    kb = jnp.where(c == 1, lon, (lon + LONS - 1) % LONS)
    east = (kb + 1) % LONS
    q = (1 - r) * 2 + (1 - c)
    edge = lat == (LATS - 1 if r == 1 else 0)
    if p == 0:
        va = lat if r == 1 else jnp.where(edge, 0, lat - 1)
        slot1 = edge if r == 0 else None
        pos0, pos1 = q, 4 + q - 2
    else:
        va = lat if r == 0 else jnp.where(edge, lat, lat + 1)
        slot1 = None if r == 0 else jnp.logical_not(edge)
        pos0, pos1 = q + 2, 4 + q
    zero = window_host(va, kb, 0)
    one = window_host(va, east, 1)
    if slot1 is None:
        (hlat, hlon), pos = (zero, pos0) if p == 0 else (one, pos1)
    else:
        hlat, hlon = jnp.where(slot1, one[0], zero[0]), jnp.where(slot1, one[1], zero[1])
        pos = jnp.where(slot1, pos1, pos0)
    relayed = jnp.logical_and(kb % 4 == 3, va % 2 == 1)
    return hlat, hlon, pos, relayed


def inbox_source(lat, lon, slot, q):
    va, vb = window_of(lat, lon, slot)
    south, east = q // 2, q % 2
    if slot == 0:
        edge = va == LATS - 1
        if south == 0:
            slat, r, p = va, 1, 0
        else:
            slat = jnp.where(edge, va, va + 1)
            r = jnp.where(edge, 1, 0)
            p = jnp.where(edge, 1, 0)
        slon = (vb + east) % LONS
    else:
        edge = va == 0
        if south == 1:
            slat, r, p = va, 0, 1
        else:
            slat = jnp.where(edge, va, va - 1)
            r = jnp.where(edge, 0, 1)
            p = jnp.where(edge, 0, 1)
        slon = (vb + LONS - 1 + east) % LONS
    return slat, slon, (r * 2 + (1 - east)) * 2 + p


def grid_row(m):
    tail = m >= 256
    k = jnp.where(tail, (m - 256) >> 2, m >> 5)
    t = jnp.where(tail, 32 + ((m - 256) & 3), m & 31)
    r, c, p = k >> 2, (k >> 1) & 1, k & 1
    l2 = jnp.where(t >= 18, 1, 0)
    t = t - 18 * l2
    r3 = jnp.where(t >= 6, 1, 0) + jnp.where(t >= 12, 1, 0)
    lev = (1 + 2 * p + l2) & 3
    return ((3 * r + r3) * 12 + 6 * c + t - 6 * r3) * 4 + lev


def tail_map(count, j):
    rows = iota((4 * count, 1), 0)
    return ones_where((rows >> 2) * 16 + 4 * j + (rows & 3) == iota((4 * count, 16 * count), 1))


def store_blocks(ref, base, rows, count):
    for k in range(count):
        ref[base + k, :, 0:512] = rows[32 * k : 32 * k + 16]
        ref[base + k, :, 512:1024] = rows[32 * k + 16 : 32 * k + 32]
    tails = rows[32 * count :]
    packed = sum(
        dot(tail_map(count, j), tails[:, 128 * j : 128 * j + 128], 0, 0) for j in range(4)
    ).astype(BF)
    for k in range(count):
        ref[base + k, :, 1024:1152] = packed[16 * k : 16 * k + 16]


def load_blocks(ref, base, count):
    main = []
    for k in range(count):
        main += [ref[base + k, :, 0:512], ref[base + k, :, 512:1024]]
    packed = jnp.concatenate([ref[base + k, :, 1024:1152] for k in range(count)], 0)
    tails = jnp.concatenate([dot(tail_map(count, j), packed) for j in range(4)], 1).astype(BF)
    return jnp.concatenate(main + [tails], 0)


def group_ids(m, slot, edge):
    tail = m >= 128
    q = jnp.where(tail, (m - 128) >> 2, m >> 5)
    t = jnp.where(tail, 32 + ((m - 128) & 3), m & 31)
    l2 = jnp.where(t >= 18, 1, 0)
    south = q >> 1
    first = jnp.where(edge, south * (1 + l2), 0)
    second = jnp.where(edge, jnp.where(south == 0, 2, l2), l2)
    return jnp.where(slot == 0, first, second)


def kernel(
    factor,
    fields_hbm, qkv_hbm, out_hbm, cot_hbm,
    layer_ref, grad_ref, dw_ref,
    raw, wide_f, wide_c, hat, inv, dw_t, qkv_w, out_w,
    out_f, out_c, in_f, in_c, res_b, res_g, ret_b, ret_g, rel_f, rel_c,
    proj, att, ctx, cots, gctx, gproj, acc,
    a_src, a_dst, b_src, b_dst, c_src, c_dst, d_src, d_dst,
    w_sem, sf, sc, sb, sg, rf, rc, rb, rg, tf, tc, uf, uc,
    a_sem, bs_sem, br_sem, cs_sem, cr_sem, ds_sem, dr_sem, ring_sem,
):
    lat = lax.axis_index("lat")
    lon = lax.axis_index("lon")
    core, zl = lat % 2, lat // 2
    y, h, x = lon // 8, (lon // 4) % 2, lon % 4
    z = h * 8 + zl
    yx = y * 4 + x
    collector = zl // 2 == x

    def at(y_, x_, z_, c_):
        return ((z_ % 8) * 2 + c_, y_ * 8 + (z_ // 8) * 4 + x_)

    def same(dlat, dlon):
        return jnp.logical_and(dlat == lat, dlon == lon)

    load_x = [
        pltpu.make_async_copy(fields_hbm, raw.at[0], w_sem.at[0]),
        pltpu.make_async_copy(cot_hbm, raw.at[1], w_sem.at[1]),
    ]
    load_w = [
        pltpu.make_async_copy(qkv_hbm, qkv_w, w_sem.at[2]),
        pltpu.make_async_copy(out_hbm, out_w, w_sem.at[3]),
    ]
    for copy in load_x + load_w:
        copy.start()

    far = jnp.where(x >= 2, 1, 0)
    hosts = []
    for j in range(8):
        r, p, c = (j >> 1) & 1, j & 1, far if j < 4 else 1 - far
        hosts.append(((r * 2 + c) * 2 + p,) + block_host(lat, lon, r, c, p))
    sources = [inbox_source(lat, lon, i // 4, i % 4) for i in range(8)]
    outer = lon + 2 * far - 1
    inner = lon + 1 - 2 * far
    relays = jnp.logical_or(x == 1, x == 2)
    passed = []
    for j in range(4):
        hlat, hlon, pos, relayed = block_host(lat, jnp.where(relays, outer, lon), (j >> 1) & 1, far, j & 1)
        passed.append((jnp.logical_and(relays, relayed), hlat, hlon, pos))

    barrier = pltpu.get_barrier_semaphore()

    def tell(dlat, dlon):
        pl.semaphore_signal(barrier, inc=1, device_id=(dlat, dlon), device_id_type=MESH)

    due = jnp.int32(16)
    for slat, slon, k in sources:
        cross = (jnp.where((k & 2) != 0, slon, slon + LONS - 1) % 4) == 3
        by = jnp.logical_and(cross, lat % 2 == 1)
        slon = slon + jnp.where(by, jnp.where(slon % 4 == 3, -1, 1), 0)
        pl.when(jnp.logical_not(same(slat, slon)))(functools.partial(tell, slat, slon))
    for j, (_, hlat, hlon, _, relayed) in enumerate(hosts):
        due = due + jnp.where(same(hlat, hlon), 0, 1)
    for flag, *_ in passed:
        due = due + jnp.where(flag, 1, 0)
        pl.when(flag)(functools.partial(tell, lat, outer))
    for d in (4, 12):
        tell(*at(y, x, (z + d) % 16, core))

    @pl.when(collector)
    def _():
        for d in (3, 13, 2, 14, 1, 15):
            tell(*at(y, x, (z + d) % 16, core))

    for collecting in (0, 1, 8, 9):
        away = (2 * x + collecting - z + 16) % 16
        due = due + jnp.where((away >= 1) & (away <= 3) | (away >= 13), 1, 0)

    def tell_plane(d, carry):
        partner = yx ^ d
        tell(*at(partner // 4, partner % 4, z, core))
        return carry

    lax.fori_loop(1, 16, tell_plane, 0)
    tell(zl * 2 + 1 - core, lon)

    due = due + 2

    to_blocks = ones_where(grid_row(iota((288, 1), 0)) == iota((288, 288), 1))
    load_x[0].wait()
    for i in range(72):
        wide_f[4 * i : 4 * i + 4] = raw[0, i].astype(F32)
    wide = wide_f[...]
    centred = wide - jnp.mean(wide, -1, keepdims=True)
    inverse = lax.rsqrt(jnp.mean(centred * centred, -1, keepdims=True) + EPSILON)
    normed_hat = centred * inverse
    hat[...] = normed_hat
    inv[...] = inverse
    store_blocks(out_f, 0, dot(to_blocks, normed_hat.astype(BF)).astype(BF), 8)
    load_x[1].wait()
    for i in range(72):
        wide_c[4 * i : 4 * i + 4] = raw[1, i].astype(F32)
    store_blocks(out_c, 0, dot(to_blocks, wide_c[...].astype(BF)).astype(BF), 8)

    pl.semaphore_wait(barrier, due)
    for d in (4, 12):
        pl.semaphore_signal(
            ring_sem, inc=1, device_id=at(y, x, (z + d) % 16, core), device_id_type=MESH
        )

    def send(src, dst, send_sems, recv_sems, i, dlat, dlon, j):
        here = same(dlat, dlon)

        @pl.when(here)
        def _():
            pltpu.make_async_copy(src.at[i], dst.at[j], recv_sems.at[j]).start()

        @pl.when(jnp.logical_not(here))
        def _():
            pltpu.make_async_remote_copy(
                src_ref=src.at[i], dst_ref=dst.at[j], send_sem=send_sems.at[i], recv_sem=recv_sems.at[j],
                device_id=(dlat, dlon), device_id_type=MESH,
            ).start()

    def landed(dst, sems, j):
        pltpu.make_async_copy(dst.at[j], dst.at[j], sems.at[j]).wait()

    def sent(src, sems, i, dlat, dlon):
        @pl.when(jnp.logical_not(same(dlat, dlon)))
        def _():
            pltpu.make_async_copy(src.at[i], src.at[i], sems.at[i]).wait()

    def relay_copy(src, dst, send_sems, recv_sems, k, j):
        return pltpu.make_async_remote_copy(
            src_ref=src.at[k], dst_ref=dst.at[j], send_sem=send_sems.at[k], recv_sem=recv_sems.at[j],
            device_id=(lat, inner), device_id_type=MESH,
        )

    halo = ((out_f, in_f, rel_f, sf, rf, tf, uf), (out_c, in_c, rel_c, sc, rc, tc, uc))
    for src, dst, rel, ss, rs, ts, us in halo:
        for j, (k, hlat, hlon, pos, relayed) in enumerate(hosts[:4]):
            pl.when(relayed)(lambda: relay_copy(src, rel, ss, ts, k, j).start())
            pl.when(jnp.logical_not(relayed))(lambda: send(src, dst, ss, rs, k, hlat, hlon, pos))
    for src, dst, rel, ss, rs, ts, us in halo:
        for k, hlat, hlon, pos, _ in hosts[4:]:
            send(src, dst, ss, rs, k, hlat, hlon, pos)
    for src, dst, rel, ss, rs, ts, us in halo:
        for j, (flag, hlat, hlon, pos) in enumerate(passed):
            @pl.when(flag)
            def _():
                landed(rel, ts, j)
                pltpu.make_async_remote_copy(
                    src_ref=rel.at[j], dst_ref=dst.at[pos], send_sem=us.at[j], recv_sem=rs.at[pos],
                    device_id=(hlat, hlon), device_id_type=MESH,
                ).start()

    for copy in load_w:
        copy.wait()

    first_half = iota((144, 128), 1) < 64

    def halves(pair):
        zero = jnp.zeros_like(pair)
        return jnp.concatenate([jnp.where(first_half, pair, zero), jnp.where(first_half, zero, pair)], 0)

    def merge(stacked):
        return jnp.where(first_half, stacked[:144], stacked[144:])

    def send_back(slot, src, dst, ss, rs):
        def go(s):
            for q in range(4):
                slat, slon, k = sources[s * 4 + q]
                send(src, dst, ss, rs, s * 4 + q, slat, slon, k)

        if isinstance(slot, int):
            go(slot)
        else:
            for s in range(2):
                pl.when(slot == s)(functools.partial(go, s))

    def a_copy():
        return pltpu.make_async_remote_copy(
            src_ref=a_src, dst_ref=a_dst, send_sem=a_sem.at[0], recv_sem=a_sem.at[1],
            device_id=(zl * 2 + 1 - core, lon), device_id_type=MESH,
        )

    def core_to_plane():
        a_copy().wait()
        for x_ in range(4):
            both = acc[2 * x_ : 2 * x_ + 2, core] + a_dst[2 * x_ : 2 * x_ + 2].astype(F32)
            both = both.astype(BF).reshape(64, D)
            for y_ in range(4):
                b_src[y_ * 4 + x_] = both[:, 128 * y_ : 128 * y_ + 128]

        for d in FAR_FIRST:
            partner = yx ^ d
            pltpu.make_async_remote_copy(
                src_ref=b_src.at[partner], dst_ref=b_dst.at[yx], send_sem=bs_sem.at[partner], recv_sem=br_sem.at[yx],
                device_id=at(partner // 4, partner % 4, z, core), device_id_type=MESH,
            ).start()
        b_dst[yx] = b_src[yx]

    def plane_to_ring():
        def wait(d, carry):
            partner = yx ^ d
            pltpu.make_async_copy(b_dst.at[partner], b_dst.at[partner], br_sem.at[partner]).wait()
            return carry

        lax.fori_loop(1, 16, wait, 0)
        c_src[...] = jnp.sum(b_dst[...].astype(F32), 0).astype(BF).reshape(2, 32, 128)
        pl.semaphore_wait(ring_sem, 2)
        for t in range(4):
            z_ = (t // 2) * 8 + 2 * x + t % 2

            @pl.when(z_ != z)
            def _():
                pltpu.make_async_remote_copy(
                    src_ref=c_src.at[t % 2], dst_ref=c_dst.at[z], send_sem=cs_sem.at[t], recv_sem=cr_sem.at[z],
                    device_id=at(y, x, z_, core), device_id_type=MESH,
                ).start()

    edges = [window_of(lat, lon, 0)[0] == LATS - 1, window_of(lat, lon, 1)[0] == 0]

    def slot_of(i):
        return jnp.where(x == 3 - core, 1 - i, i)

    def forward(i, carry):
        slot = slot_of(i)
        edge = jnp.where(slot == 0, edges[0], edges[1])
        for q in range(4):
            landed(in_f, rf, slot * 4 + q)
        proj[slot] = dot(load_blocks(in_f, slot * 4, 4), qkv_w[...]).astype(BF)
        allowed = group_ids(iota((144, 1), 0), slot, edge) == group_ids(iota((1, 144), 1), slot, edge)
        allowed = jnp.concatenate([allowed, allowed], 0)
        for g in range(4):
            lanes = slice(128 * g, 128 * g + 128)
            query = halves(proj[slot, :, lanes])
            key = proj[slot, :, 512 + 128 * g : 640 + 128 * g]
            value = proj[slot, :, 1024 + 128 * g : 1152 + 128 * g]
            scores = jnp.where(allowed, dot(query, key, 1, 1) * 0.125, MASK_FILL)
            lifted = jnp.exp(scores - jnp.max(scores, -1, keepdims=True))
            attend = lifted * (1.0 / jnp.sum(lifted, -1, keepdims=True))
            att[slot * 4 + g] = attend
            ctx[slot, :, lanes] = merge(dot(attend.astype(BF), value)).astype(BF)
        return carry

    lax.fori_loop(0, 2, forward, 0)

    for i in range(2):
        slot = slot_of(i)
        for q in range(4):
            landed(in_c, rc, slot * 4 + q)
        cots[slot] = load_blocks(in_c, slot * 4, 4)
    both_ctx = ctx[...].reshape(288, D)
    both_cot = cots[...].reshape(288, D)
    acc[...] = (dot(both_ctx, both_cot, 0, 0) * factor).reshape(8, 2, 32, D)
    a_src[...] = acc[:, 1 - core].astype(BF)
    a_copy().start()

    gctx[...] = dot(both_cot, out_w[...], 1, 1).astype(BF).reshape(2, 144, D)
    core_to_plane()
    branch = dot(ctx[...].reshape(288, D), out_w[...]).astype(BF)
    for slot in range(2):
        store_blocks(res_b, slot * 4, branch[144 * slot : 144 * slot + 144], 4)
        send_back(slot, res_b, ret_b, sb, rb)

    def backward(i, carry):
        slot = slot_of(i)
        for g in range(4):
            lanes = slice(128 * g, 128 * g + 128)
            query = halves(proj[slot, :, lanes])
            key = proj[slot, :, 512 + 128 * g : 640 + 128 * g]
            value = proj[slot, :, 1024 + 128 * g : 1152 + 128 * g]
            grad_out = halves(gctx[slot, :, lanes])
            attend = att[slot * 4 + g]
            grad_att = dot(grad_out, value, 1, 1)
            total = jnp.sum(attend * grad_att, -1, keepdims=True)
            grad_scores = (attend * (grad_att - total) * 0.125).astype(BF)
            gproj[:, lanes] = merge(dot(grad_scores, key)).astype(BF)
            gproj[:, 512 + 128 * g : 640 + 128 * g] = dot(grad_scores, query, 0, 0).astype(BF)
            gproj[:, 1024 + 128 * g : 1152 + 128 * g] = dot(attend.astype(BF), grad_out, 0, 0).astype(BF)
        store_blocks(res_g, slot * 4, dot(gproj[...], qkv_w[...], 1, 1).astype(BF), 4)
        send_back(slot, res_g, ret_g, sg, rg)
        return carry

    lax.fori_loop(0, 2, backward, 0)
    plane_to_ring()

    @pl.when(collector)
    def _():
        c_dst[z] = c_src[zl % 2]

        def c_wait(d, carry):
            partner = z ^ d
            pltpu.make_async_copy(c_dst.at[partner], c_dst.at[partner], cr_sem.at[partner]).wait()
            return carry

        lax.fori_loop(1, 16, c_wait, 0)
        d_src[...] = jnp.sum(c_dst[...].astype(F32), 0)
        for d in range(1, 4):
            pltpu.make_async_remote_copy(
                src_ref=d_src, dst_ref=d_dst, send_sem=ds_sem.at[d], recv_sem=dr_sem,
                device_id=at(y, x ^ d, z, core), device_id_type=MESH,
            ).start()

    for k in range(8):
        landed(ret_b, rb, k)
    from_blocks = ones_where(grid_row(iota((1, 288), 1)) == iota((288, 288), 0))
    wide_f[...] += dot(from_blocks, load_blocks(ret_b, 0, 8))
    for i in range(72):
        layer_ref[i] = wide_f[4 * i : 4 * i + 4].astype(BF)
    for k in range(8):
        landed(ret_g, rg, k)
    grad = dot(from_blocks, load_blocks(ret_g, 0, 8))
    normed_hat = hat[...]
    centred = grad - jnp.mean(grad, -1, keepdims=True)
    wide_c[...] += inv[...] * (centred - normed_hat * jnp.mean(grad * normed_hat, -1, keepdims=True))
    for i in range(72):
        grad_ref[i] = wide_c[4 * i : 4 * i + 4].astype(BF)

    @pl.when(jnp.logical_not(collector))
    def _():
        pltpu.make_async_copy(d_dst, d_dst, dr_sem).wait()

    dw_t[...] = jnp.where(collector, d_src[...], d_dst[...]).T
    dw_ref[...] = dw_t[pl.ds(pl.multiple_of(16 * (h * 4 + x), 16), 16)]

    def b_sent(d, carry):
        partner = yx ^ d
        pltpu.make_async_copy(b_src.at[partner], b_src.at[partner], bs_sem.at[partner]).wait()
        return carry

    lax.fori_loop(1, 16, b_sent, 0)
    for src, dst, rel, ss, rs, ts, us in halo:
        for k, hlat, hlon, _, _ in hosts:
            sent(src, ss, k, hlat, hlon)
        for j, (flag, *_) in enumerate(passed):
            pl.when(flag)(lambda: pltpu.make_async_copy(rel.at[j], rel.at[j], us.at[j]).wait())
    for i, (slat, slon, _) in enumerate(sources):
        sent(res_b, sb, i, slat, slon)
        sent(res_g, sg, i, slat, slon)
    for t in range(4):
        z_ = (t // 2) * 8 + 2 * x + t % 2

        @pl.when(z_ != z)
        def _():
            pltpu.make_async_copy(c_src.at[t % 2], c_src.at[t % 2], cs_sem.at[t]).wait()

    @pl.when(collector)
    def _():
        for d in range(1, 4):
            pltpu.make_async_copy(d_src, d_src, ds_sem.at[d]).wait()


def on_device(fields, qkv_weight, out_weight, cotangent):
    grid_shape = fields.shape
    tokens = fields.size // D * lax.axis_size("lat") * lax.axis_size("lon")
    factor = 1.0 / math.sqrt(tokens)
    vmem = pl.BlockSpec(memory_space=pltpu.VMEM)
    hbm = pl.BlockSpec(memory_space=pltpu.HBM)
    dma = pltpu.SemaphoreType.DMA
    layer, grad, dw = pl.pallas_call(
        functools.partial(kernel, factor),
        out_shape=[
            pltpu.VMEM((72, 4, D), BF),
            pltpu.VMEM((72, 4, D), BF),
            pltpu.VMEM((16, 32), F32),
        ],
        in_specs=[hbm, hbm, hbm, hbm],
        out_specs=[vmem, vmem, vmem],
        scratch_shapes=[
            pltpu.VMEM((2, 72, 4, D), BF),
            pltpu.VMEM((288, D), F32),
            pltpu.VMEM((288, D), F32),
            pltpu.VMEM((288, D), F32),
            pltpu.VMEM((288, 1), F32),
            pltpu.VMEM((128, 32), F32),
            pltpu.VMEM((D, 3 * D), BF),
            pltpu.VMEM((D, D), BF),
        ]
        + [pltpu.VMEM((8,) + BLOCK, BF)] * 8
        + [pltpu.VMEM((4,) + BLOCK, BF)] * 2
        + [
            pltpu.VMEM((2, 144, 3 * D), BF),
            pltpu.VMEM((8, 288, 144), F32),
            pltpu.VMEM((2, 144, D), BF),
            pltpu.VMEM((2, 144, D), BF),
            pltpu.VMEM((2, 144, D), BF),
            pltpu.VMEM((144, 3 * D), BF),
            pltpu.VMEM((8, 2, 32, D), F32),
            pltpu.VMEM((8, 32, D), BF),
            pltpu.VMEM((8, 32, D), BF),
            pltpu.VMEM((16, 64, 128), BF),
            pltpu.VMEM((16, 64, 128), BF),
            pltpu.VMEM((2, 32, 128), BF),
            pltpu.VMEM((16, 32, 128), BF),
            pltpu.VMEM((32, 128), F32),
            pltpu.VMEM((32, 128), F32),
            dma((4,)),
        ]
        + [dma((8,))] * 8
        + [dma((4,))] * 4
        + [dma((2,)), dma((16,)), dma((16,)), dma((4,)), dma((16,)), dma((4,)), dma, pltpu.SemaphoreType.REGULAR],
        compiler_params=pltpu.CompilerParams(
            collective_id=0, has_side_effects=True, vmem_limit_bytes=VMEM_LIMIT
        ),
        cost_estimate=pl.CostEstimate(flops=1_600_000_000, bytes_accessed=4_000_000, transcendentals=400_000),
        name="window_attention",
    )(by_place(fields), qkv_weight, out_weight, by_place(cotangent))
    return from_place(layer, grid_shape), from_place(grad, grid_shape), dw.T


def by_place(grid):
    return grid.transpose(1, 2, 0, 3).reshape(72, 4, D)


def from_place(tokens, grid_shape):
    lev, lat, lon, d = grid_shape
    return tokens.reshape(lat, lon, lev, d).transpose(2, 0, 1, 3)


def solution(mesh):
    in_specs = (P(None, "lat", "lon", None), P(), P(), P(None, "lat", "lon", None))
    out_specs = (P(None, "lat", "lon", None), P(None, "lat", "lon", None), P("lat", "lon"))
    return jax.shard_map(
        on_device, mesh=mesh, in_specs=in_specs, out_specs=out_specs, check_vma=False
    )
```

```python
import functools
import math

import jax
import jax.numpy as jnp
from jax import lax
from jax.experimental import pallas as pl
from jax.experimental.pallas import tpu as pltpu
from jax.sharding import PartitionSpec as P

MESH = pl.DeviceIdType.MESH
EPSILON = 1e-05
MASK_FILL = -1e30
BF = jnp.bfloat16
F32 = jnp.float32
D = 512
LATS = 16
LONS = 32
VMEM_LIMIT = 60 * 2**20
BLOCK = (16, 1152)


def dot(a, b, ca=1, cb=0):
    return lax.dot_general(a, b, (((ca,), (cb,)), ((), ())), preferred_element_type=F32)


def iota(shape, dim):
    return lax.broadcasted_iota(jnp.int32, shape, dim)


def ones_where(cond):
    return jnp.where(cond, 1.0, 0.0).astype(BF)


def z_quarter(lat, lon, back):
    zl = lat // 2
    h = (lon // 4) % 2
    low = (zl + 4) % 8
    wraps = 1 - zl // 4 if back else zl // 4
    return low * 2 + lat % 2, lon + ((h + wraps) % 2 - h) * 4


def moved(lat, lon, cond, back):
    qlat, qlon = z_quarter(lat, lon, back)
    return jnp.where(cond, qlat, lat), jnp.where(cond, qlon, lon)


def window_host(va, vb, slot):
    x = vb % 4
    odd = va % 2
    crossing = x == (3 if slot == 0 else 0)
    inner = x == (2 if slot == 0 else 1)
    step = 1 - 2 * slot
    hlat, hlon = moved(va, vb, crossing, False)
    shift = jnp.where(crossing, -step, jnp.where(inner, step, 0)) * odd
    return hlat, hlon + shift


def window_of(lat, lon, slot):
    x = lon % 4
    odd = lat % 2
    crossing = x == (3 - odd if slot == 0 else odd)
    inner = jnp.logical_and(x == (3 if slot == 0 else 0), odd == 1)
    step = 1 - 2 * slot
    vlat, vlon = moved(lat, lon, crossing, True)
    shift = jnp.where(crossing, step, jnp.where(inner, -step, 0)) * odd
    return vlat, vlon + shift


def block_host(lat, lon, r, c, p):
    kb = jnp.where(c == 1, lon, (lon + LONS - 1) % LONS)
    east = (kb + 1) % LONS
    q = (1 - r) * 2 + (1 - c)
    edge = lat == (LATS - 1 if r == 1 else 0)
    if p == 0:
        va = lat if r == 1 else jnp.where(edge, 0, lat - 1)
        slot1 = edge if r == 0 else None
        pos0, pos1 = q, 4 + q - 2
    else:
        va = lat if r == 0 else jnp.where(edge, lat, lat + 1)
        slot1 = None if r == 0 else jnp.logical_not(edge)
        pos0, pos1 = q + 2, 4 + q
    zero = window_host(va, kb, 0)
    one = window_host(va, east, 1)
    if slot1 is None:
        (hlat, hlon), pos = (zero, pos0) if p == 0 else (one, pos1)
    else:
        hlat, hlon = jnp.where(slot1, one[0], zero[0]), jnp.where(slot1, one[1], zero[1])
        pos = jnp.where(slot1, pos1, pos0)
    relayed = jnp.logical_and(kb % 4 == 3, va % 2 == 1)
    return hlat, hlon, pos, relayed


def inbox_source(lat, lon, slot, q):
    va, vb = window_of(lat, lon, slot)
    south, east = q // 2, q % 2
    if slot == 0:
        edge = va == LATS - 1
        if south == 0:
            slat, r, p = va, 1, 0
        else:
            slat = jnp.where(edge, va, va + 1)
            r = jnp.where(edge, 1, 0)
            p = jnp.where(edge, 1, 0)
        slon = (vb + east) % LONS
    else:
        edge = va == 0
        if south == 1:
            slat, r, p = va, 0, 1
        else:
            slat = jnp.where(edge, va, va - 1)
            r = jnp.where(edge, 0, 1)
            p = jnp.where(edge, 0, 1)
        slon = (vb + LONS - 1 + east) % LONS
    return slat, slon, (r * 2 + (1 - east)) * 2 + p


def grid_row(m):
    tail = m >= 256
    k = jnp.where(tail, (m - 256) >> 2, m >> 5)
    t = jnp.where(tail, 32 + ((m - 256) & 3), m & 31)
    r, c, p = k >> 2, (k >> 1) & 1, k & 1
    l2 = jnp.where(t >= 18, 1, 0)
    t = t - 18 * l2
    r3 = jnp.where(t >= 6, 1, 0) + jnp.where(t >= 12, 1, 0)
    lev = (1 + 2 * p + l2) & 3
    return ((3 * r + r3) * 12 + 6 * c + t - 6 * r3) * 4 + lev


def tail_map(count, j):
    rows = iota((4 * count, 1), 0)
    return ones_where((rows >> 2) * 16 + 4 * j + (rows & 3) == iota((4 * count, 16 * count), 1))


def store_blocks(ref, base, rows, count):
    for k in range(count):
        ref[base + k, :, 0:512] = rows[32 * k : 32 * k + 16]
        ref[base + k, :, 512:1024] = rows[32 * k + 16 : 32 * k + 32]
    tails = rows[32 * count :]
    packed = sum(
        dot(tail_map(count, j), tails[:, 128 * j : 128 * j + 128], 0, 0) for j in range(4)
    ).astype(BF)
    for k in range(count):
        ref[base + k, :, 1024:1152] = packed[16 * k : 16 * k + 16]


def load_blocks(ref, base, count):
    main = []
    for k in range(count):
        main += [ref[base + k, :, 0:512], ref[base + k, :, 512:1024]]
    packed = jnp.concatenate([ref[base + k, :, 1024:1152] for k in range(count)], 0)
    tails = jnp.concatenate([dot(tail_map(count, j), packed) for j in range(4)], 1).astype(BF)
    return jnp.concatenate(main + [tails], 0)


def group_ids(m, slot, edge):
    tail = m >= 128
    q = jnp.where(tail, (m - 128) >> 2, m >> 5)
    t = jnp.where(tail, 32 + ((m - 128) & 3), m & 31)
    l2 = jnp.where(t >= 18, 1, 0)
    south = q >> 1
    first = jnp.where(edge, south * (1 + l2), 0)
    second = jnp.where(edge, jnp.where(south == 0, 2, l2), l2)
    return jnp.where(slot == 0, first, second)


def kernel(
    factor,
    fields_hbm, qkv_hbm, out_hbm, cot_hbm,
    layer_ref, grad_ref, dw_ref,
    raw, wide_f, wide_c, hat, inv, dw_t, qkv_w, out_w,
    out_f, out_c, in_f, in_c, res_b, res_g, ret_b, ret_g, rel_f, rel_c,
    proj, att, ctx, cots, gctx, gproj, acc,
    a_src, a_dst, b_src, b_dst, c_src, c_dst, d_src, d_dst,
    w_sem, sf, sc, sb, sg, rf, rc, rb, rg, tf, tc, uf, uc,
    a_sem, bs_sem, br_sem, cs_sem, cr_sem, ds_sem, dr_sem, ring_sem,
):
    lat = lax.axis_index("lat")
    lon = lax.axis_index("lon")
    core, zl = lat % 2, lat // 2
    y, h, x = lon // 8, (lon // 4) % 2, lon % 4
    z = h * 8 + zl
    yx = y * 4 + x
    collector = zl // 2 == x

    def at(y_, x_, z_, c_):
        return ((z_ % 8) * 2 + c_, y_ * 8 + (z_ // 8) * 4 + x_)

    def same(dlat, dlon):
        return jnp.logical_and(dlat == lat, dlon == lon)

    load_x = [
        pltpu.make_async_copy(fields_hbm, raw.at[0], w_sem.at[0]),
        pltpu.make_async_copy(cot_hbm, raw.at[1], w_sem.at[1]),
    ]
    load_w = [
        pltpu.make_async_copy(qkv_hbm, qkv_w, w_sem.at[2]),
        pltpu.make_async_copy(out_hbm, out_w, w_sem.at[3]),
    ]
    for copy in load_x + load_w:
        copy.start()

    sources = [inbox_source(lat, lon, i // 4, i % 4) for i in range(8)]
    barrier = pltpu.get_barrier_semaphore()

    def tell(dlat, dlon):
        pl.semaphore_signal(barrier, inc=1, device_id=(dlat, dlon), device_id_type=MESH)

    due = jnp.int32(16)
    for slat, slon, k in sources:
        cross = (jnp.where((k & 2) != 0, slon, slon + LONS - 1) % 4) == 3
        by = jnp.logical_and(cross, lat % 2 == 1)
        slon = slon + jnp.where(by, jnp.where(slon % 4 == 3, -1, 1), 0)
        pl.when(jnp.logical_not(same(slat, slon)))(functools.partial(tell, slat, slon))
    far = jnp.where(x >= 2, 1, 0)
    hosts = []
    for j in range(8):
        r, p, c = (j >> 1) & 1, j & 1, far if j < 4 else 1 - far
        hosts.append(((r * 2 + c) * 2 + p,) + block_host(lat, lon, r, c, p))
    outer = lon + 2 * far - 1
    inner = lon + 1 - 2 * far
    relays = jnp.logical_or(x == 1, x == 2)
    passed = []
    for j in range(4):
        hlat, hlon, pos, relayed = block_host(lat, jnp.where(relays, outer, lon), (j >> 1) & 1, far, j & 1)
        passed.append((jnp.logical_and(relays, relayed), hlat, hlon, pos))

    for j, (_, hlat, hlon, _, relayed) in enumerate(hosts):
        due = due + jnp.where(same(hlat, hlon), 0, 1)
    for flag, *_ in passed:
        due = due + jnp.where(flag, 1, 0)
        pl.when(flag)(functools.partial(tell, lat, outer))
    for d in (4, 12):
        tell(*at(y, x, (z + d) % 16, core))

    @pl.when(collector)
    def _():
        for d in (3, 13, 2, 14, 1, 15):
            tell(*at(y, x, (z + d) % 16, core))

    for collecting in (0, 1, 8, 9):
        away = (2 * x + collecting - z + 16) % 16
        due = due + jnp.where((away >= 1) & (away <= 3) | (away >= 13), 1, 0)

    def tell_plane(d, carry):
        partner = yx ^ d
        tell(*at(partner // 4, partner % 4, z, core))
        return carry

    lax.fori_loop(1, 16, tell_plane, 0)
    tell(zl * 2 + 1 - core, lon)

    due = due + 2

    to_blocks = ones_where(grid_row(iota((288, 1), 0)) == iota((288, 288), 1))
    load_x[0].wait()
    for i in range(72):
        wide_f[4 * i : 4 * i + 4] = raw[0, i].astype(F32)
    wide = wide_f[...]
    centred = wide - jnp.mean(wide, -1, keepdims=True)
    inverse = lax.rsqrt(jnp.mean(centred * centred, -1, keepdims=True) + EPSILON)
    normed_hat = centred * inverse
    hat[...] = normed_hat
    inv[...] = inverse
    store_blocks(out_f, 0, dot(to_blocks, normed_hat.astype(BF)).astype(BF), 8)
    load_x[1].wait()
    for i in range(72):
        wide_c[4 * i : 4 * i + 4] = raw[1, i].astype(F32)
    store_blocks(out_c, 0, dot(to_blocks, wide_c[...].astype(BF)).astype(BF), 8)

    pl.semaphore_wait(barrier, due)
    for d in (4, 12):
        pl.semaphore_signal(
            ring_sem, inc=1, device_id=at(y, x, (z + d) % 16, core), device_id_type=MESH
        )

    def send(src, dst, send_sems, recv_sems, i, dlat, dlon, j):
        here = same(dlat, dlon)

        @pl.when(here)
        def _():
            pltpu.make_async_copy(src.at[i], dst.at[j], recv_sems.at[j]).start()

        @pl.when(jnp.logical_not(here))
        def _():
            pltpu.make_async_remote_copy(
                src_ref=src.at[i], dst_ref=dst.at[j], send_sem=send_sems.at[i], recv_sem=recv_sems.at[j],
                device_id=(dlat, dlon), device_id_type=MESH,
            ).start()

    def landed(dst, sems, j):
        pltpu.make_async_copy(dst.at[j], dst.at[j], sems.at[j]).wait()

    def sent(src, sems, i, dlat, dlon):
        @pl.when(jnp.logical_not(same(dlat, dlon)))
        def _():
            pltpu.make_async_copy(src.at[i], src.at[i], sems.at[i]).wait()

    def relay_copy(src, dst, send_sems, recv_sems, k, j):
        return pltpu.make_async_remote_copy(
            src_ref=src.at[k], dst_ref=dst.at[j], send_sem=send_sems.at[k], recv_sem=recv_sems.at[j],
            device_id=(lat, inner), device_id_type=MESH,
        )

    halo = ((out_f, in_f, rel_f, sf, rf, tf, uf), (out_c, in_c, rel_c, sc, rc, tc, uc))
    for src, dst, rel, ss, rs, ts, us in halo:
        for j, (k, hlat, hlon, pos, relayed) in enumerate(hosts[:4]):
            pl.when(relayed)(lambda: relay_copy(src, rel, ss, ts, k, j).start())
        for k, hlat, hlon, pos, relayed in hosts[:4]:
            pl.when(jnp.logical_not(relayed))(lambda: send(src, dst, ss, rs, k, hlat, hlon, pos))
    for src, dst, rel, ss, rs, ts, us in halo:
        for k, hlat, hlon, pos, _ in hosts[4:]:
            send(src, dst, ss, rs, k, hlat, hlon, pos)
    for src, dst, rel, ss, rs, ts, us in halo:
        for j, (flag, hlat, hlon, pos) in enumerate(passed):
            @pl.when(flag)
            def _():
                landed(rel, ts, j)
                pltpu.make_async_remote_copy(
                    src_ref=rel.at[j], dst_ref=dst.at[pos], send_sem=us.at[j], recv_sem=rs.at[pos],
                    device_id=(hlat, hlon), device_id_type=MESH,
                ).start()

    for copy in load_w:
        copy.wait()

    first_half = iota((144, 128), 1) < 64

    def halves(pair):
        zero = jnp.zeros_like(pair)
        return jnp.concatenate([jnp.where(first_half, pair, zero), jnp.where(first_half, zero, pair)], 0)

    def merge(stacked):
        return jnp.where(first_half, stacked[:144], stacked[144:])

    def send_back(slot, src, dst, ss, rs):
        def go(s):
            for q in range(4):
                slat, slon, k = sources[s * 4 + q]
                send(src, dst, ss, rs, s * 4 + q, slat, slon, k)

        if isinstance(slot, int):
            go(slot)
        else:
            for s in range(2):
                pl.when(slot == s)(functools.partial(go, s))

    def a_copy(part):
        rows = pl.ds(2 * part, 2)
        return pltpu.make_async_remote_copy(
            src_ref=a_src.at[rows], dst_ref=a_dst.at[rows], send_sem=a_sem.at[part], recv_sem=a_sem.at[4 + part],
            device_id=(zl * 2 + 1 - core, lon), device_id_type=MESH,
        )

    def core_to_plane():
        for dx in (2, 1, 3, 0):
            x_ = x ^ dx
            a_copy(x_).wait()
            rows = pl.ds(2 * x_, 2)
            both = acc[rows, core] + a_dst[rows].astype(F32)
            both = both.astype(BF).reshape(64, D)
            for y_ in range(4):
                b_src[y_ * 4 + x_] = both[:, 128 * y_ : 128 * y_ + 128]
            for dy in (2, 1, 3, 0):
                if dx + dy:
                    partner = (y ^ dy) * 4 + x_
                    pltpu.make_async_remote_copy(
                        src_ref=b_src.at[partner], dst_ref=b_dst.at[yx],
                        send_sem=bs_sem.at[partner], recv_sem=br_sem.at[yx],
                        device_id=at(y ^ dy, x_, z, core), device_id_type=MESH,
                    ).start()
        b_dst[yx] = b_src[yx]

    def plane_to_ring():
        def wait(d, carry):
            partner = yx ^ d
            pltpu.make_async_copy(b_dst.at[partner], b_dst.at[partner], br_sem.at[partner]).wait()
            return carry

        lax.fori_loop(1, 16, wait, 0)
        c_src[...] = jnp.sum(b_dst[...].astype(F32), 0).astype(BF).reshape(2, 32, 128)
        pl.semaphore_wait(ring_sem, 2)
        for t in range(4):
            z_ = (t // 2) * 8 + 2 * x + t % 2

            @pl.when(z_ != z)
            def _():
                pltpu.make_async_remote_copy(
                    src_ref=c_src.at[t % 2], dst_ref=c_dst.at[z], send_sem=cs_sem.at[t], recv_sem=cr_sem.at[z],
                    device_id=at(y, x, z_, core), device_id_type=MESH,
                ).start()

    edges = [window_of(lat, lon, 0)[0] == LATS - 1, window_of(lat, lon, 1)[0] == 0]

    def slot_of(i):
        return jnp.where(x == 3 - core, 1 - i, i)

    def forward(i, carry):
        slot = slot_of(i)
        edge = jnp.where(slot == 0, edges[0], edges[1])
        for q in range(4):
            landed(in_f, rf, slot * 4 + q)
        proj[slot] = dot(load_blocks(in_f, slot * 4, 4), qkv_w[...]).astype(BF)
        allowed = group_ids(iota((144, 1), 0), slot, edge) == group_ids(iota((1, 144), 1), slot, edge)
        allowed = jnp.concatenate([allowed, allowed], 0)
        for g in range(4):
            lanes = slice(128 * g, 128 * g + 128)
            query = halves(proj[slot, :, lanes])
            key = proj[slot, :, 512 + 128 * g : 640 + 128 * g]
            value = proj[slot, :, 1024 + 128 * g : 1152 + 128 * g]
            scores = jnp.where(allowed, dot(query, key, 1, 1) * 0.125, MASK_FILL)
            lifted = jnp.exp(scores - jnp.max(scores, -1, keepdims=True))
            attend = lifted * (1.0 / jnp.sum(lifted, -1, keepdims=True))
            att[slot * 4 + g] = attend
            ctx[slot, :, lanes] = merge(dot(attend.astype(BF), value)).astype(BF)
        return carry

    lax.fori_loop(0, 2, forward, 0)

    for i in range(2):
        slot = slot_of(i)
        for q in range(4):
            landed(in_c, rc, slot * 4 + q)
        cots[slot] = load_blocks(in_c, slot * 4, 4)
    both_ctx = ctx[...].reshape(288, D)
    both_cot = cots[...].reshape(288, D)
    acc[...] = (dot(both_ctx, both_cot, 0, 0) * factor).reshape(8, 2, 32, D)
    for dx in (2, 1, 3, 0):
        rows = pl.ds(2 * (x ^ dx), 2)
        a_src[rows] = acc[rows, 1 - core].astype(BF)
        a_copy(x ^ dx).start()

    gctx[...] = dot(both_cot, out_w[...], 1, 1).astype(BF).reshape(2, 144, D)
    core_to_plane()
    branch = dot(ctx[...].reshape(288, D), out_w[...]).astype(BF)
    for slot in range(2):
        store_blocks(res_b, slot * 4, branch[144 * slot : 144 * slot + 144], 4)
        send_back(slot, res_b, ret_b, sb, rb)

    def backward(i, carry):
        slot = slot_of(i)
        for g in range(4):
            lanes = slice(128 * g, 128 * g + 128)
            query = halves(proj[slot, :, lanes])
            key = proj[slot, :, 512 + 128 * g : 640 + 128 * g]
            value = proj[slot, :, 1024 + 128 * g : 1152 + 128 * g]
            grad_out = halves(gctx[slot, :, lanes])
            attend = att[slot * 4 + g]
            grad_att = dot(grad_out, value, 1, 1)
            total = jnp.sum(attend * grad_att, -1, keepdims=True)
            grad_scores = (attend * (grad_att - total) * 0.125).astype(BF)
            gproj[:, lanes] = merge(dot(grad_scores, key)).astype(BF)
            gproj[:, 512 + 128 * g : 640 + 128 * g] = dot(grad_scores, query, 0, 0).astype(BF)
            gproj[:, 1024 + 128 * g : 1152 + 128 * g] = dot(attend.astype(BF), grad_out, 0, 0).astype(BF)
        store_blocks(res_g, slot * 4, dot(gproj[...], qkv_w[...], 1, 1).astype(BF), 4)
        send_back(slot, res_g, ret_g, sg, rg)
        return carry

    lax.fori_loop(0, 2, backward, 0)
    plane_to_ring()

    @pl.when(collector)
    def _():
        c_dst[z] = c_src[zl % 2]

        def c_wait(d, carry):
            partner = z ^ d
            pltpu.make_async_copy(c_dst.at[partner], c_dst.at[partner], cr_sem.at[partner]).wait()
            return carry

        lax.fori_loop(1, 16, c_wait, 0)
        d_src[...] = jnp.sum(c_dst[...].astype(F32), 0)
        for d in range(1, 4):
            pltpu.make_async_remote_copy(
                src_ref=d_src, dst_ref=d_dst, send_sem=ds_sem.at[d], recv_sem=dr_sem,
                device_id=at(y, x ^ d, z, core), device_id_type=MESH,
            ).start()

    for k in range(8):
        landed(ret_b, rb, k)
    from_blocks = ones_where(grid_row(iota((1, 288), 1)) == iota((288, 288), 0))
    wide_f[...] += dot(from_blocks, load_blocks(ret_b, 0, 8))
    for i in range(72):
        layer_ref[i] = wide_f[4 * i : 4 * i + 4].astype(BF)
    for k in range(8):
        landed(ret_g, rg, k)
    grad = dot(from_blocks, load_blocks(ret_g, 0, 8))
    normed_hat = hat[...]
    centred = grad - jnp.mean(grad, -1, keepdims=True)
    wide_c[...] += inv[...] * (centred - normed_hat * jnp.mean(grad * normed_hat, -1, keepdims=True))
    for i in range(72):
        grad_ref[i] = wide_c[4 * i : 4 * i + 4].astype(BF)

    @pl.when(jnp.logical_not(collector))
    def _():
        pltpu.make_async_copy(d_dst, d_dst, dr_sem).wait()

    dw_t[...] = jnp.where(collector, d_src[...], d_dst[...]).T
    dw_ref[...] = dw_t[pl.ds(pl.multiple_of(16 * (h * 4 + x), 16), 16)]

    def b_sent(d, carry):
        partner = yx ^ d
        pltpu.make_async_copy(b_src.at[partner], b_src.at[partner], bs_sem.at[partner]).wait()
        return carry

    lax.fori_loop(1, 16, b_sent, 0)
    for src, dst, rel, ss, rs, ts, us in halo:
        for k, hlat, hlon, _, _ in hosts:
            sent(src, ss, k, hlat, hlon)
        for j, (flag, *_) in enumerate(passed):
            pl.when(flag)(lambda: pltpu.make_async_copy(rel.at[j], rel.at[j], us.at[j]).wait())
    for i, (slat, slon, _) in enumerate(sources):
        sent(res_b, sb, i, slat, slon)
        sent(res_g, sg, i, slat, slon)
    for t in range(4):
        z_ = (t // 2) * 8 + 2 * x + t % 2

        @pl.when(z_ != z)
        def _():
            pltpu.make_async_copy(c_src.at[t % 2], c_src.at[t % 2], cs_sem.at[t]).wait()

    @pl.when(collector)
    def _():
        for d in range(1, 4):
            pltpu.make_async_copy(d_src, d_src, ds_sem.at[d]).wait()


def on_device(fields, qkv_weight, out_weight, cotangent):
    grid_shape = fields.shape
    tokens = fields.size // D * lax.axis_size("lat") * lax.axis_size("lon")
    factor = 1.0 / math.sqrt(tokens)
    vmem = pl.BlockSpec(memory_space=pltpu.VMEM)
    hbm = pl.BlockSpec(memory_space=pltpu.HBM)
    dma = pltpu.SemaphoreType.DMA
    layer, grad, dw = pl.pallas_call(
        functools.partial(kernel, factor),
        out_shape=[
            pltpu.VMEM((72, 4, D), BF),
            pltpu.VMEM((72, 4, D), BF),
            pltpu.VMEM((16, 32), F32),
        ],
        in_specs=[hbm, hbm, hbm, hbm],
        out_specs=[vmem, vmem, vmem],
        scratch_shapes=[
            pltpu.VMEM((2, 72, 4, D), BF),
            pltpu.VMEM((288, D), F32),
            pltpu.VMEM((288, D), F32),
            pltpu.VMEM((288, D), F32),
            pltpu.VMEM((288, 1), F32),
            pltpu.VMEM((128, 32), F32),
            pltpu.VMEM((D, 3 * D), BF),
            pltpu.VMEM((D, D), BF),
        ]
        + [pltpu.VMEM((8,) + BLOCK, BF)] * 8
        + [pltpu.VMEM((4,) + BLOCK, BF)] * 2
        + [
            pltpu.VMEM((2, 144, 3 * D), BF),
            pltpu.VMEM((8, 288, 144), F32),
            pltpu.VMEM((2, 144, D), BF),
            pltpu.VMEM((2, 144, D), BF),
            pltpu.VMEM((2, 144, D), BF),
            pltpu.VMEM((144, 3 * D), BF),
            pltpu.VMEM((8, 2, 32, D), F32),
            pltpu.VMEM((8, 32, D), BF),
            pltpu.VMEM((8, 32, D), BF),
            pltpu.VMEM((16, 64, 128), BF),
            pltpu.VMEM((16, 64, 128), BF),
            pltpu.VMEM((2, 32, 128), BF),
            pltpu.VMEM((16, 32, 128), BF),
            pltpu.VMEM((32, 128), F32),
            pltpu.VMEM((32, 128), F32),
            dma((4,)),
        ]
        + [dma((8,))] * 8
        + [dma((4,))] * 4
        + [dma((8,)), dma((16,)), dma((16,)), dma((4,)), dma((16,)), dma((4,)), dma, pltpu.SemaphoreType.REGULAR],
        compiler_params=pltpu.CompilerParams(
            collective_id=0, has_side_effects=True, vmem_limit_bytes=VMEM_LIMIT
        ),
        cost_estimate=pl.CostEstimate(flops=1_600_000_000, bytes_accessed=4_000_000, transcendentals=400_000),
        name="window_attention",
    )(by_place(fields), qkv_weight, out_weight, by_place(cotangent))
    return from_place(layer, grid_shape), from_place(grad, grid_shape), dw.T


def by_place(grid):
    return grid.transpose(1, 2, 0, 3).reshape(72, 4, D)


def from_place(tokens, grid_shape):
    lev, lat, lon, d = grid_shape
    return tokens.reshape(lat, lon, lev, d).transpose(2, 0, 1, 3)


def solution(mesh):
    in_specs = (P(None, "lat", "lon", None), P(), P(), P(None, "lat", "lon", None))
    out_specs = (P(None, "lat", "lon", None), P(None, "lat", "lon", None), P("lat", "lon"))
    return jax.shard_map(
        on_device, mesh=mesh, in_specs=in_specs, out_specs=out_specs, check_vma=False
    )
```
